128 devices in a mesh: query: 4 (over y_lo, core), corpus: 32 (over z, y_hi, x).
Axes of the slice: x: 4, y: 4 (y_hi: 2, y_lo: 2; y = y_hi * 2 + y_lo), z: 4, core: 2. Of those that a mesh axis runs over, the one named last changes fastest.
Arguments:
- queries: bfloat16 [1024, 32, 128], P('corpus', 'query'), may hold values from -6 to 6
- passages: bfloat16 [1024, 128, 128], P(('query', 'corpus')), may hold values from -0.5 to 0.5
- lengths: int32 [1024], P(('query', 'corpus')), may hold values from 8 to 128, as said below
Outputs:
- scores: float32 [1024, 1024], P('corpus', 'query')
The draws below stay inside these ranges and needn't reach their ends.
Inputs may be any that keep to these rules, and one draw needn't show every extreme that they name: `lengths`: every length is a multiple of 8; some passage uses all 128 slots.
All inputs are finite; a program needn't handle non-finite values.
Results may differ from the reference program's by a relative error of at most 0.0003.
Values may be sent and summed in bfloat16 or wider, within the bound.
No kernel may reach another device: no remote copies, remote signals or barrier semaphores. Data moves between devices by JAX's collectives and lax.ppermute only.
A program may use at most 64 MiB of HBM per device.

```python
import jax
import jax.numpy as jnp
from jax import lax

D = 128
QT = 32
L = 128
QUERIES = 1024
PASSAGES = 1024


def draw_lengths(key, part):
    key = jax.random.fold_in(key, 5)
    first_key, second_key = jax.random.split(key)
    values = 8 * jax.random.randint(first_key, (PASSAGES,), 1, L // 8 + 1)
    chosen = jax.random.randint(second_key, (), 0, PASSAGES)
    places = jnp.arange(PASSAGES, dtype=jnp.int32)
    return jnp.where(places == chosen, L, values).astype(jnp.int32)


def shard_levels(own_key, extent, shards, least, top_value):
    def one(dim, parts):
        draws = jax.random.uniform(jax.random.fold_in(jax.random.fold_in(own_key, 6), dim), (parts,), jnp.float32, least / len(shards), top_value / len(shards))
        return jnp.repeat(jnp.exp(draws), extent[dim] // parts).reshape((-1,) + (1,) * (len(extent) - dim - 1))

    level = one(*shards[0])
    for cut in shards[1:]:
        level = level * one(*cut)
    return level


def scatter_about(key, extent, deviation, limit, cuts=(), held_as=jnp.bfloat16):
    factor_of = shard_levels(key, extent, cuts, -0.22, 0.18) if cuts else 1.0
    drawn = jax.random.normal(key, extent, jnp.float32) * deviation * factor_of
    return jnp.minimum(jnp.maximum(drawn, -limit), limit).astype(held_as)


def setup_inputs(seed: int = 0) -> dict:
    arg_keys = jax.random.split(jax.random.key(seed), 4)
    return {
        "queries": scatter_about(arg_keys[0], (QUERIES, QT, D), 1.0, 6.0, ((0, 32), (1, 4))),
        "passages": scatter_about(arg_keys[1], (PASSAGES, L, D), D ** -0.5, 0.5, ((0, 128),)),
        "lengths": draw_lengths(jax.random.fold_in(arg_keys[3], 71), 0),
    }


masked_value = -1.0e30


def block_scores(flat_rows, piece, piece_lengths, query_len):
    count = piece.shape[0]
    slots = piece.shape[1]
    width = piece.shape[2]
    row_count = flat_rows.shape[0]
    dots = lax.dot_general(flat_rows, piece.reshape(count * slots, width), (((1,), (1,)), ((), ())), preferred_element_type=jnp.float32)
    dots = dots.reshape(row_count, count, slots)
    usable = lax.broadcasted_iota(jnp.int32, (count, slots), 1) < piece_lengths[:, None]
    top_dot = jnp.max(jnp.where(usable[None], dots, masked_value), axis=2)
    return jnp.mean(top_dot.reshape(row_count // query_len, query_len, count), axis=1)


def reference(queries, passages, lengths):
    flat_rows = queries.reshape(QUERIES * QT, D)

    def one_block(pieces):
        return block_scores(flat_rows, pieces[0], pieces[1], QT)

    blocks = lax.map(one_block, (passages.reshape(PASSAGES // 8, 8, L, D), lengths.reshape(PASSAGES // 8, 8)))
    return jnp.transpose(blocks, (1, 0, 2)).reshape(QUERIES, PASSAGES)
```

```python
import functools

import jax
import jax.numpy as jnp
from jax import lax
from jax.experimental import pallas as pl
from jax.experimental.pallas import tpu as pltpu
from jax.sharding import Mesh
from jax.sharding import PartitionSpec as P

NAMES = ("ylo", "core", "z", "yhi", "x")
SIZES = (2, 2, 4, 2, 4)
PLANE = ("ylo", "core", "z", "yhi")
SHIFTS = (0, 1, -1, 2)


def plane_pairs(move):
    def index(ylo, core, z, yhi):
        return ((ylo * 2 + core) * 4 + z) * 2 + yhi

    pairs = []
    for ylo in range(2):
        for core in range(2):
            for z in range(4):
                for yhi in range(2):
                    y2, core2, z2 = move(2 * yhi + ylo, core, z)
                    y2, z2 = y2 % 4, z2 % 4
                    pairs.append((index(ylo, core, z, yhi), index(y2 % 2, core2, z2, y2 // 2)))
    return pairs


def along(first, shift):
    def move(y, core, z):
        if (core == 0) == first:
            return y + shift, core, z
        return y, core, z + shift

    return plane_pairs(move)


def to_core(v):
    return lax.ppermute(v, "core", [(0, 1), (1, 0)])


def on_x(v, shift):
    return lax.ppermute(v, "x", [(i, (i + shift) % 4) for i in range(4)])


def fill_kernel(len_ref, p_ref, o_ref):
    slot = lax.broadcasted_iota(jnp.int32, p_ref.shape[1:], 0)
    for i in range(p_ref.shape[0]):
        v = p_ref[i].astype(jnp.float32)
        o_ref[i] = jnp.where(slot < len_ref[i], v, v[0:1]).astype(o_ref.dtype)


def fill(passages, lengths):
    return pl.pallas_call(
        fill_kernel,
        out_shape=jax.ShapeDtypeStruct(passages.shape, passages.dtype),
        in_specs=[pl.BlockSpec(memory_space=pltpu.SMEM), pl.BlockSpec(memory_space=pltpu.VMEM)],
        out_specs=pl.BlockSpec(memory_space=pltpu.VMEM),
    )(lengths, passages)


def dot_nt(a, b, precision=None):
    return lax.dot_general(
        a, b, (((1,), (1,)), ((), ())), preferred_element_type=jnp.float32, precision=precision
    )


def score_kernel(info_ref, *refs):
    rows, pieces, out_ref, acc_ref = refs[:8], refs[8:12], refs[12], refs[13]
    z, y, core, x = info_ref[0], info_ref[1], info_ref[2], info_ref[3]
    acc_ref[...] = jnp.zeros_like(acc_ref)
    for a in range(8):
        kind = core if a < 4 else 1 - core
        far = SHIFTS[a % 4]
        w = rows[a][...].reshape(1024, 128)
        places = []
        for j in range(4):
            near = SHIFTS[j]
            y_from = lax.rem(y + 4 - jnp.where(kind == 0, near, far), 4)
            z_from = lax.rem(z + 4 - jnp.where(kind == 0, far, near), 4)
            places.append(z_from * 2 + y_from // 2)
        for m in range(4):
            p_ref = pieces[m]
            g = pl.multiple_of(8 * lax.rem(x + 4 - SHIFTS[m], 4), 8)
            tops = []
            for i in range(8):
                d = dot_nt(p_ref[i], w)
                tops.append(jnp.max(d.reshape(16, 8, 1024), axis=0)[None])
            top = jnp.max(jnp.concatenate(tops, axis=0), axis=1)
            for j in range(4):
                acc_ref[places[j], pl.ds(g, 8), :] += top[:, 256 * j : 256 * j + 256]
    lane = lax.broadcasted_iota(jnp.int32, (32, 256), 1)
    row = lax.broadcasted_iota(jnp.int32, (32, 256), 0)
    pick = jnp.where(lane // 8 == row, 1.0 / 32, 0.0).astype(jnp.float32)
    for c in range(8):
        r = dot_nt(pick, acc_ref[c], lax.Precision.HIGHEST)
        out_ref[c] = jnp.concatenate([r[0:8], r[8:16], r[16:24], r[24:32]], axis=1)


def score(info, rows, pieces):
    return pl.pallas_call(
        score_kernel,
        out_shape=jax.ShapeDtypeStruct((8, 8, 128), jnp.float32),
        in_specs=[pl.BlockSpec(memory_space=pltpu.SMEM)]
        + [pl.BlockSpec(memory_space=pltpu.VMEM)] * 12,
        out_specs=pl.BlockSpec(memory_space=pltpu.VMEM),
        scratch_shapes=[pltpu.VMEM((8, 32, 256), jnp.float32)],
        compiler_params=pltpu.CompilerParams(vmem_limit_bytes=48 << 20),
    )(info, *rows, *pieces)


def place_kernel(r_ref, o_ref):
    for g in range(4):
        o_ref[8 * g : 8 * g + 8, :] = jnp.concatenate(
            [r_ref[s][:, 32 * g : 32 * g + 32] for s in range(8)], axis=1
        )


def place(received):
    return pl.pallas_call(
        place_kernel,
        out_shape=jax.ShapeDtypeStruct((32, 256), jnp.float32),
        in_specs=[pl.BlockSpec(memory_space=pltpu.VMEM)],
        out_specs=pl.BlockSpec(memory_space=pltpu.VMEM),
    )(received)


def per_device(queries, passages, lengths):
    own = queries.reshape(256, 128)
    z = lax.axis_index("z")
    y = lax.axis_index("yhi") * 2 + lax.axis_index("ylo")
    core = lax.axis_index("core")
    x = lax.axis_index("x")
    info = jnp.stack([z, y, core, x]).astype(jnp.int32)

    near = [own] + [lax.ppermute(own, PLANE, along(True, k)) for k in SHIFTS[1:]]
    filled = fill(passages, lengths)
    moved = [filled] + [on_x(filled, k) for k in SHIFTS[1:]]
    block = jnp.stack(near)
    mine = [block] + [lax.ppermute(block, PLANE, along(False, k)) for k in SHIFTS[1:]]
    other = [to_core(v) for v in mine]
    terms = score(info, mine + other, moved)
    received = lax.all_to_all(terms, ("z", "yhi"), 0, 0, tiled=True)
    return place(received)


def solution(mesh):
    fine = Mesh(mesh.devices.reshape(SIZES), NAMES)
    corpus = ("z", "yhi", "x")
    query = ("ylo", "core")
    return jax.shard_map(
        per_device,
        mesh=fine,
        in_specs=(P(corpus, query, None), P(query + corpus, None, None), P(query + corpus)),
        out_specs=P(corpus, query),
        check_vma=False,
    )
```

```python
import jax
import jax.numpy as jnp
from jax import lax
from jax.experimental import pallas as pl
from jax.experimental.pallas import tpu as pltpu
from jax.sharding import Mesh
from jax.sharding import PartitionSpec as P

NAMES = ("ylo", "core", "z", "yhi", "x")
SIZES = (2, 2, 4, 2, 4)
SHIFTS = (0, 1, -1, 2)
FROM = tuple((k, flip) for k in SHIFTS for flip in range(2))


def on_y(v, shift):
    def index(y):
        return (y % 2) * 2 + y // 2

    return lax.ppermute(v, ("ylo", "yhi"), [(index(i), index((i + shift) % 4)) for i in range(4)])


def on_z(v, shift):
    return lax.ppermute(v, "z", [(i, (i + shift) % 4) for i in range(4)])


def on_z_yhi(v, shift, flip):
    pairs = [
        (z * 2 + yhi, ((z + shift) % 4) * 2 + (yhi ^ flip)) for z in range(4) for yhi in range(2)
    ]
    return lax.ppermute(v, ("z", "yhi"), pairs)


def to_core(v):
    return lax.ppermute(v, "core", [(0, 1), (1, 0)])


def on_x(v, shift):
    return lax.ppermute(v, "x", [(i, (i + shift) % 4) for i in range(4)])


def fill_kernel(len_ref, p_ref, o_ref):
    slot = lax.broadcasted_iota(jnp.int32, p_ref.shape[1:], 0)
    for i in range(p_ref.shape[0]):
        v = p_ref[i].astype(jnp.float32)
        o_ref[i] = jnp.where(slot < len_ref[i], v, v[0:1]).astype(o_ref.dtype)


def fill(passages, lengths):
    return pl.pallas_call(
        fill_kernel,
        out_shape=jax.ShapeDtypeStruct(passages.shape, passages.dtype),
        in_specs=[pl.BlockSpec(memory_space=pltpu.SMEM), pl.BlockSpec(memory_space=pltpu.VMEM)],
        out_specs=pl.BlockSpec(memory_space=pltpu.VMEM),
    )(lengths, passages)


def dot_nt(a, b, precision=None):
    return lax.dot_general(
        a, b, (((1,), (1,)), ((), ())), preferred_element_type=jnp.float32, precision=precision
    )


def score_kernel(info_ref, mine_ref, other_ref, *refs):
    pieces, outs, acc_ref = refs[:4], refs[4:6], refs[6]
    x, ylo = info_ref[0], info_ref[1]
    mate = 2 - ylo
    lane = lax.broadcasted_iota(jnp.int32, (32, 256), 1)
    row = lax.broadcasted_iota(jnp.int32, (32, 256), 0)
    pick = jnp.where(lane // 8 == row, 1.0 / 32, 0.0).astype(jnp.float32)
    for half, pair in ((1, (3 - mate, 3)), (0, (0, mate))):
        w = jnp.concatenate([ref[j] for ref in (mine_ref, other_ref) for j in pair], axis=0)
        for m in range(4):
            tops = []
            for i in range(8):
                d = dot_nt(pieces[m][i], w)
                tops.append(jnp.max(d.reshape(16, 8, 1024), axis=0)[None])
            top = jnp.max(jnp.concatenate(tops, axis=0), axis=1)
            total = top[:, 0:256] + top[:, 256:512] + top[:, 512:768] + top[:, 768:1024]
            place = pl.multiple_of(8 * lax.rem(x + 4 - SHIFTS[m], 4), 8)
            acc_ref[pl.ds(place, 8), :] = total
        r = dot_nt(pick, acc_ref[...], lax.Precision.HIGHEST)
        outs[half][...] = jnp.concatenate([r[0:8], r[8:16], r[16:24], r[24:32]], axis=1)


def score(info, mine, other, pieces):
    return pl.pallas_call(
        score_kernel,
        out_shape=[jax.ShapeDtypeStruct((8, 128), jnp.float32)] * 2,
        in_specs=[pl.BlockSpec(memory_space=pltpu.SMEM)]
        + [pl.BlockSpec(memory_space=pltpu.VMEM)] * 6,
        out_specs=[pl.BlockSpec(memory_space=pltpu.VMEM)] * 2,
        scratch_shapes=[pltpu.VMEM((32, 256), jnp.float32)],
        compiler_params=pltpu.CompilerParams(vmem_limit_bytes=32 << 20),
        cost_estimate=pl.CostEstimate(
            flops=2 * 2048 * 4096 * 128 * 2, bytes_accessed=1 << 20, transcendentals=0
        ),
    )(info, mine, other, *pieces)


def place_kernel(info_ref, *refs):
    parts, o_ref, held_ref = refs[:8], refs[8], refs[9]
    z, yhi = info_ref[2], info_ref[3]
    for n, (shift, flip) in enumerate(FROM):
        source = lax.rem(z + 4 + shift, 4) * 2 + (yhi if flip == 0 else 1 - yhi)
        held_ref[source] = parts[n][...]
    for g in range(4):
        o_ref[8 * g : 8 * g + 8, :] = jnp.concatenate(
            [held_ref[s][:, 32 * g : 32 * g + 32] for s in range(8)], axis=1
        )


def place(info, parts):
    return pl.pallas_call(
        place_kernel,
        out_shape=jax.ShapeDtypeStruct((32, 256), jnp.float32),
        in_specs=[pl.BlockSpec(memory_space=pltpu.SMEM)]
        + [pl.BlockSpec(memory_space=pltpu.VMEM)] * 8,
        out_specs=pl.BlockSpec(memory_space=pltpu.VMEM),
        scratch_shapes=[pltpu.VMEM((8, 8, 128), jnp.float32)],
    )(info, *parts)


def per_device(queries, passages, lengths):
    own = queries.reshape(256, 128)
    places = [lax.axis_index(name) for name in ("x", "ylo", "z", "yhi")]
    info = jnp.stack(places).astype(jnp.int32)

    near = [own] + [on_y(own, k) for k in SHIFTS[1:]]
    filled = fill(passages, lengths)
    pieces = [filled] + [on_x(filled, k) for k in SHIFTS[1:]]
    block = jnp.stack(near)
    parts = []
    for k in SHIFTS:
        mine = block if k == 0 else on_z(block, k)
        terms = score(info, mine, to_core(mine), pieces)
        for flip in range(2):
            parts.append(terms[flip] if (k, flip) == (0, 0) else on_z_yhi(terms[flip], -k, flip))
    return place(info, parts)


def solution(mesh):
    fine = Mesh(mesh.devices.reshape(SIZES), NAMES)
    corpus = ("z", "yhi", "x")
    query = ("ylo", "core")
    return jax.shard_map(
        per_device,
        mesh=fine,
        in_specs=(P(corpus, query, None), P(query + corpus, None, None), P(query + corpus)),
        out_specs=P(corpus, query),
        check_vma=False,
    )
```

```python
import functools

import jax
import jax.numpy as jnp
from jax import lax
from jax.experimental import pallas as pl
from jax.experimental.pallas import tpu as pltpu
from jax.sharding import Mesh
from jax.sharding import PartitionSpec as P

NAMES = ("ylo", "core", "z", "yhi", "x")
SIZES = (2, 2, 4, 2, 4)
PLANE = ("ylo", "core", "z", "yhi")
SHIFTS = (0, 1, -1, 2)
OWN, SLOTS, WIDTH = 8, 128, 128
DEPTH = 16
LOWEST = -3.0e38


def plane_pairs(move):
    def index(ylo, core, z, yhi):
        return ((ylo * 2 + core) * 4 + z) * 2 + yhi

    pairs = []
    for ylo in range(2):
        for core in range(2):
            for z in range(4):
                for yhi in range(2):
                    y2, core2, z2 = move(2 * yhi + ylo, core, z)
                    y2, z2 = y2 % 4, z2 % 4
                    pairs.append((index(ylo, core, z, yhi), index(y2 % 2, core2, z2, y2 // 2)))
    return pairs


def along(first, shift):
    def move(y, core, z):
        if (core == 0) == first:
            return y + shift, core, z
        return y, core, z + shift

    return plane_pairs(move)


def to_core(v):
    return lax.ppermute(v, "core", [(0, 1), (1, 0)])


def on_x(v, shift):
    return lax.ppermute(v, "x", [(i, (i + shift) % 4) for i in range(4)])


def fill_kernel(len_ref, p_ref, o_ref):
    slot = lax.broadcasted_iota(jnp.int32, (SLOTS, WIDTH), 0)
    lane = lax.broadcasted_iota(jnp.int32, (16, WIDTH), 1)
    lengths = jnp.zeros((16, WIDTH), jnp.float32)
    for i in range(OWN):
        v = p_ref[i].astype(jnp.float32)
        o_ref[SLOTS * i : SLOTS * i + SLOTS, :] = jnp.where(slot < len_ref[i], v, v[0:1]).astype(o_ref.dtype)
        lengths = jnp.where(lane == i, len_ref[i].astype(jnp.float32), lengths)
    o_ref[OWN * SLOTS :, :] = lengths.astype(o_ref.dtype)


def fill(passages, lengths):
    return pl.pallas_call(
        fill_kernel,
        out_shape=jax.ShapeDtypeStruct((OWN * SLOTS + 16, WIDTH), passages.dtype),
        in_specs=[pl.BlockSpec(memory_space=pltpu.SMEM), pl.BlockSpec(memory_space=pltpu.VMEM)],
        out_specs=pl.BlockSpec(memory_space=pltpu.VMEM),
    )(lengths, passages)


def merge(values, sublane):
    step = 1
    while len(values) > 1:
        low = (sublane & step) == 0
        joined = []
        for a, b in zip(values[0::2], values[1::2]):
            kept, moved = jnp.where(low, a, b), jnp.where(low, b, a)
            joined.append(jnp.maximum(kept, pltpu.roll(moved, step, 0)))
        values = joined
        step *= 2
    return values[0]


def best_dots(w_ref, p_ref, m_ref, s_ref, unit_ref, turns, *acc):
    acc = (acc[:DEPTH], acc[DEPTH:])
    m_ref[...] = jnp.full_like(m_ref, LOWEST)
    nothing = jnp.zeros((16, 128), jnp.bfloat16)

    def push(g):
        for u in range(2):
            pltpu.matmul_push_rhs(w_ref[g * 2 + u], 0, u, transpose=True)

    def issue(unit, j, fresh=False):
        slots = p_ref[pl.ds(pl.multiple_of(unit, 16), 16), :]
        lhs = jnp.concatenate(
            [
                jnp.concatenate([slots, nothing], axis=1),
                jnp.concatenate([nothing, slots], axis=1),
            ],
            axis=0,
        )
        for u in range(2):
            pltpu.matmul_acc_lhs(acc[u][j], lhs, load_staged_rhs=0 if fresh else None)

    def take(unit, j):
        p = lax.shift_right_logical(unit, 7)
        for u in range(2):
            d = pltpu.matmul_pop(acc[u][j])
            for half in range(2):
                top = jnp.maximum(d[16 * half : 16 * half + 8], d[16 * half + 8 : 16 * half + 16])
                m_ref[p, 2 * u + half] = jnp.maximum(m_ref[p, 2 * u + half], top)

    push(0)
    for j in range(DEPTH):
        issue(unit_ref[j], j, fresh=j == 0)

    def group(g, carry):
        push(jnp.minimum(g + 1, 7))

        def turn(t, c):
            for j in range(DEPTH):
                take(unit_ref[t * DEPTH + j], j)
                issue(unit_ref[t * DEPTH + DEPTH + j], j)
            return c

        lax.fori_loop(0, turns - 1, turn, 0)
        last = (turns - 1) * DEPTH
        for j in range(DEPTH):
            take(unit_ref[last + j], j)
            issue(unit_ref[j], j, fresh=j == 0)
        sublane = lax.broadcasted_iota(jnp.int32, (8, 256), 0)
        lowest = jnp.full((8, 256), LOWEST, jnp.float32)
        for o in range(4):
            total = None
            for b in range(4):
                top = merge([m_ref[8 * o + i, b] for i in range(8)], sublane)
                for i in range(8):
                    m_ref[8 * o + i, b] = lowest
                total = top if total is None else total + top
            s_ref[g, 8 * o : 8 * o + 8, :] = total
        return carry

    lax.fori_loop(0, 8, group, 0)
    for u in range(2):
        for j in range(DEPTH):
            m_ref[0, 0] = pltpu.matmul_pop(acc[u][j])[0:8]


def score_kernel(info_ref, *refs):
    rows, pieces, out_ref = refs[:8], refs[8:12], refs[12]
    w_ref, p_ref, m_ref, s_ref, unit_ref = refs[13:]
    z, yhi, core, x, ylo = (info_ref[i] for i in range(5))
    mate = 2 - ylo

    for kind in range(2):

        @pl.when(core == kind)
        def _():
            for a in range(8):
                for j in range(4):
                    same = (a < 4) == (kind == 0)
                    dz, dy = (a % 4, j) if same else (j, a % 4)
                    h = {0: 0, 3: 1}.get(dy, (mate != dy).astype(jnp.int32))
                    half = 128 * (dy in (1, 2))
                    w_ref[(dz * 2 + h) * 2 + a // 4, :, half : half + 128] = rows[a][j]

    count = jnp.int32(0)
    for m in range(4):
        from_x = lax.rem(x + 4 - SHIFTS[m], 4)
        p_ref[pl.ds(pl.multiple_of(from_x * 1024, 1024), 1024), :] = pieces[m][0:1024, :]
        lengths = pieces[m][1024:1040, :].astype(jnp.float32)[0:8].astype(jnp.int32)
        units = lax.shift_right_logical(lengths + 15, 4)
        for i in range(OWN):
            for n in range(8):
                unit_ref[count + n] = from_x * 1024 + i * SLOTS + n * 16
            count = count + units[0, i]
    for i in range(2 * DEPTH):
        unit_ref[count + i] = unit_ref[0]
    turns = lax.div(count + DEPTH - 1, DEPTH)

    pl.run_scoped(
        functools.partial(best_dots, w_ref, p_ref, m_ref, s_ref, unit_ref, turns),
        *[pltpu.ACC(u)((32, 256), jnp.float32) for u in range(2) for _ in range(DEPTH)],
    )

    lane = lax.broadcasted_iota(jnp.int32, (32, 256), 1)
    row = lax.broadcasted_iota(jnp.int32, (32, 256), 0)
    pick = jnp.where(lane // 8 == row, 1.0 / 32, 0.0).astype(jnp.bfloat16)
    rest = s_ref[...].reshape(256, 256)
    parts = []
    for _ in range(3):
        parts.append(rest.astype(jnp.bfloat16))
        rest = rest - parts[-1].astype(jnp.float32)

    def add_up(acc):
        for part in parts:
            pltpu.matmul_push_rhs(part, 0, 0, transpose=True)
            pltpu.matmul_acc_lhs(acc, pick, load_staged_rhs=0)
        return pltpu.matmul_pop(acc)

    r = pl.run_scoped(add_up, pltpu.ACC(0)((32, 256), jnp.float32))
    for g in range(8):
        c = r[:, 32 * g : 32 * g + 32]
        place = lax.rem(z + 4 - SHIFTS[g // 2], 4) * 2 + (yhi if g % 2 == 0 else 1 - yhi)
        out_ref[place] = jnp.concatenate([c[0:8], c[8:16], c[16:24], c[24:32]], axis=1)


def score(info, rows, pieces):
    return pl.pallas_call(
        score_kernel,
        out_shape=jax.ShapeDtypeStruct((8, 8, 128), jnp.float32),
        in_specs=[pl.BlockSpec(memory_space=pltpu.SMEM)]
        + [pl.BlockSpec(memory_space=pltpu.VMEM)] * 12,
        out_specs=pl.BlockSpec(memory_space=pltpu.VMEM),
        scratch_shapes=[
            pltpu.VMEM((16, 256, 256), jnp.bfloat16),
            pltpu.VMEM((4096, 128), jnp.bfloat16),
            pltpu.VMEM((32, 4, 8, 256), jnp.float32),
            pltpu.VMEM((8, 32, 256), jnp.float32),
            pltpu.SMEM((256 + 2 * DEPTH,), jnp.int32),
        ],
        compiler_params=pltpu.CompilerParams(vmem_limit_bytes=32 << 20),
    )(info, *rows, *pieces)


def place_kernel(r_ref, o_ref):
    for g in range(4):
        o_ref[8 * g : 8 * g + 8, :] = jnp.concatenate(
            [r_ref[s][:, 32 * g : 32 * g + 32] for s in range(8)], axis=1
        )


def place(received):
    return pl.pallas_call(
        place_kernel,
        out_shape=jax.ShapeDtypeStruct((32, 256), jnp.float32),
        in_specs=[pl.BlockSpec(memory_space=pltpu.VMEM)],
        out_specs=pl.BlockSpec(memory_space=pltpu.VMEM),
    )(received)


def per_device(queries, passages, lengths):
    own = queries.reshape(256, 128)
    info = jnp.stack([lax.axis_index(name) for name in ("z", "yhi", "core", "x", "ylo")]).astype(jnp.int32)

    near = [own] + [lax.ppermute(own, PLANE, along(True, k)) for k in SHIFTS[1:]]
    filled = fill(passages, lengths)
    moved = [filled] + [on_x(filled, k) for k in SHIFTS[1:]]
    block = jnp.stack(near)
    mine = [block] + [lax.ppermute(block, PLANE, along(False, k)) for k in SHIFTS[1:]]
    other = [to_core(v) for v in mine]
    terms = score(info, mine + other, moved)
    received = lax.all_to_all(terms, ("z", "yhi"), 0, 0, tiled=True)
    return place(received)


def solution(mesh):
    fine = Mesh(mesh.devices.reshape(SIZES), NAMES)
    corpus = ("z", "yhi", "x")
    query = ("ylo", "core")
    return jax.shard_map(
        per_device,
        mesh=fine,
        in_specs=(P(corpus, query, None), P(query + corpus, None, None), P(query + corpus)),
        out_specs=P(corpus, query),
        check_vma=False,
    )
```

```python
import functools

import jax
import jax.numpy as jnp
from jax import lax
from jax.experimental import pallas as pl
from jax.experimental.pallas import tpu as pltpu
from jax.sharding import Mesh
from jax.sharding import PartitionSpec as P

NAMES = ("ylo", "core", "z", "yhi", "x")
SIZES = (2, 2, 4, 2, 4)
PLANE = ("ylo", "core", "z", "yhi")
SHIFTS = (0, 1, -1, 2)
OWN, SLOTS, WIDTH = 8, 128, 128
DEPTH = 16
LOWEST = -3.0e38


def plane_pairs(move):
    def index(ylo, core, z, yhi):
        return ((ylo * 2 + core) * 4 + z) * 2 + yhi

    pairs = []
    for ylo in range(2):
        for core in range(2):
            for z in range(4):
                for yhi in range(2):
                    y2, core2, z2 = move(2 * yhi + ylo, core, z)
                    y2, z2 = y2 % 4, z2 % 4
                    pairs.append((index(ylo, core, z, yhi), index(y2 % 2, core2, z2, y2 // 2)))
    return pairs


def along(first, shift):
    def move(y, core, z):
        if (core == 0) == first:
            return y + shift, core, z
        return y, core, z + shift

    return plane_pairs(move)


def to_core(v):
    return lax.ppermute(v, "core", [(0, 1), (1, 0)])


def on_x(v, shift):
    return lax.ppermute(v, "x", [(i, (i + shift) % 4) for i in range(4)])


def with_lengths(passages, lengths):
    tail = jnp.pad(lengths.astype(passages.dtype), (0, WIDTH - OWN))
    return jnp.concatenate(
        [passages.reshape(OWN * SLOTS, WIDTH), jnp.broadcast_to(tail, (16, WIDTH))], axis=0
    )


def best_dots(w_ref, p_ref, m_ref, s_ref, unit_ref, turns, *acc):
    acc = (acc[:DEPTH], acc[DEPTH:])
    nothing = jnp.zeros((16, 128), jnp.bfloat16)

    def push(g):
        for u in range(2):
            pltpu.matmul_push_rhs(w_ref[g * 2 + u], 0, u, transpose=True)

    def issue(unit, j, fresh=False):
        slots = p_ref[pl.ds(pl.multiple_of(unit, 16), 16), :]
        lhs = jnp.concatenate(
            [
                jnp.concatenate([slots, nothing], axis=1),
                jnp.concatenate([nothing, slots], axis=1),
            ],
            axis=0,
        )
        for u in range(2):
            pltpu.matmul_acc_lhs(acc[u][j], lhs, load_staged_rhs=0 if fresh else None)

    def take(unit, j):
        at = lax.shift_right_logical(unit, 7)
        begin = jnp.where(lax.bitwise_and(unit, 127) == 0, 32, at)
        tops = []
        held = [m_ref[b, begin] for b in range(8)]
        for u in range(2):
            d = pltpu.matmul_pop(acc[u][j])
            for half in range(2):
                top = jnp.maximum(d[16 * half : 16 * half + 8], d[16 * half + 8 : 16 * half + 16])
                tops += [top[:, 0:128], top[:, 128:256]]
        for b in range(8):
            m_ref[b, at] = jnp.maximum(held[b], tops[b])

    m_ref[:, 32] = jnp.full((8, 8, 128), LOWEST, jnp.float32)
    push(0)
    for j in range(DEPTH):
        issue(unit_ref[j], j, fresh=j == 0)

    def group(g, carry):
        push(jnp.minimum(g + 1, 7))

        def turn(t, c):
            for j in range(DEPTH):
                take(unit_ref[t * DEPTH + j], j)
                issue(unit_ref[t * DEPTH + DEPTH + j], j)
            return c

        lax.fori_loop(0, turns - 1, turn, 0)
        last = (turns - 1) * DEPTH
        for j in range(DEPTH):
            take(unit_ref[last + j], j)
            issue(unit_ref[j], j, fresh=j == 0)
        rows_ref = m_ref.reshape(8, 264, 128)
        for o in range(4):
            for side in range(2):
                total = None
                for b in range(side, 8, 2):
                    top = rows_ref[b, pl.ds(64 * o, 8, stride=8), :]
                    for i in range(1, 8):
                        top = jnp.maximum(top, rows_ref[b, pl.ds(64 * o + i, 8, stride=8), :])
                    total = top if total is None else total + top
                s_ref[g, 8 * o : 8 * o + 8, 128 * side : 128 * side + 128] = total
        return carry

    lax.fori_loop(0, 8, group, 0)
    for u in range(2):
        for j in range(DEPTH):
            m_ref[0, 0] = pltpu.matmul_pop(acc[u][j])[0:8, 0:128]


def score_kernel(info_ref, *refs):
    rows, pieces, out_ref = refs[:8], refs[8:12], refs[12]
    w_ref, p_ref, m_ref, s_ref, unit_ref = refs[13:]
    z, yhi, core, x, ylo = (info_ref[i] for i in range(5))
    mate = 2 - ylo

    for kind in range(2):

        @pl.when(core == kind)
        def _():
            for a in range(8):
                for j in range(4):
                    same = (a < 4) == (kind == 0)
                    dz, dy = (a % 4, j) if same else (j, a % 4)
                    h = {0: 0, 3: 1}.get(dy, (mate != dy).astype(jnp.int32))
                    half = 128 * (dy in (1, 2))
                    w_ref[(dz * 2 + h) * 2 + a // 4, :, half : half + 128] = rows[a][j]

    count = jnp.int32(0)
    for m in range(4):
        from_x = lax.rem(x + 4 - SHIFTS[m], 4)
        p_ref[pl.ds(pl.multiple_of(from_x * 1024, 1024), 1024), :] = pieces[m][0:1024, :]
        lengths = pieces[m][1024:1040, :].astype(jnp.float32)[0:8].astype(jnp.int32)
        units = lax.shift_right_logical(lengths + 15, 4)
        for i in range(OWN):
            for n in range(8):
                unit_ref[count + n] = from_x * 1024 + i * SLOTS + n * 16
            count = count + units[0, i]
            used = units[0, i]
            last = pl.multiple_of(from_x * 1024 + i * SLOTS + (used - 1) * 16, 16)
            both = p_ref[pl.ds(last, 16), :].astype(jnp.float32)
            second = jnp.where(lengths[0, i] == used * 16, both[8:16], both[0:8])
            p_ref[pl.ds(last, 16), :] = jnp.concatenate([both[0:8], second], axis=0).astype(p_ref.dtype)
    for i in range(DEPTH):
        unit_ref[count + i] = unit_ref[count - 1]
    turns = lax.div(count + DEPTH - 1, DEPTH)

    pl.run_scoped(
        functools.partial(best_dots, w_ref, p_ref, m_ref, s_ref, unit_ref, turns),
        *[pltpu.ACC(u)((32, 256), jnp.float32) for u in range(2) for _ in range(DEPTH)],
    )

    lane = lax.broadcasted_iota(jnp.int32, (32, 256), 1)
    row = lax.broadcasted_iota(jnp.int32, (32, 256), 0)
    pick = jnp.where(lane // 8 == row, 1.0 / 32, 0.0).astype(jnp.bfloat16)
    rest = s_ref[...].reshape(256, 256)
    parts = []
    for _ in range(3):
        parts.append(rest.astype(jnp.bfloat16))
        rest = rest - parts[-1].astype(jnp.float32)

    def add_up(acc):
        for part in parts:
            pltpu.matmul_push_rhs(part, 0, 0, transpose=True)
            pltpu.matmul_acc_lhs(acc, pick, load_staged_rhs=0)
        return pltpu.matmul_pop(acc)

    r = pl.run_scoped(add_up, pltpu.ACC(0)((32, 256), jnp.float32))
    for g in range(8):
        c = r[:, 32 * g : 32 * g + 32]
        place = lax.rem(z + 4 - SHIFTS[g // 2], 4) * 2 + (yhi if g % 2 == 0 else 1 - yhi)
        out_ref[place] = jnp.concatenate([c[0:8], c[8:16], c[16:24], c[24:32]], axis=1)


def score(info, rows, pieces):
    return pl.pallas_call(
        score_kernel,
        out_shape=jax.ShapeDtypeStruct((8, 8, 128), jnp.float32),
        in_specs=[pl.BlockSpec(memory_space=pltpu.SMEM)]
        + [pl.BlockSpec(memory_space=pltpu.VMEM)] * 12,
        out_specs=pl.BlockSpec(memory_space=pltpu.VMEM),
        scratch_shapes=[
            pltpu.VMEM((16, 256, 256), jnp.bfloat16),
            pltpu.VMEM((4096, 128), jnp.bfloat16),
            pltpu.VMEM((8, 33, 8, 128), jnp.float32),
            pltpu.VMEM((8, 32, 256), jnp.float32),
            pltpu.SMEM((256 + DEPTH,), jnp.int32),
        ],
        compiler_params=pltpu.CompilerParams(vmem_limit_bytes=32 << 20),
    )(info, *rows, *pieces)


def place_kernel(r_ref, o_ref):
    for g in range(4):
        o_ref[8 * g : 8 * g + 8, :] = jnp.concatenate(
            [r_ref[s][:, 32 * g : 32 * g + 32] for s in range(8)], axis=1
        )


def place(received):
    return pl.pallas_call(
        place_kernel,
        out_shape=jax.ShapeDtypeStruct((32, 256), jnp.float32),
        in_specs=[pl.BlockSpec(memory_space=pltpu.VMEM)],
        out_specs=pl.BlockSpec(memory_space=pltpu.VMEM),
    )(received)


def per_device(queries, passages, lengths):
    own = queries.reshape(256, 128)
    info = jnp.stack([lax.axis_index(name) for name in ("z", "yhi", "core", "x", "ylo")]).astype(jnp.int32)

    near = [own] + [lax.ppermute(own, PLANE, along(True, k)) for k in SHIFTS[1:]]
    filled = with_lengths(passages, lengths)
    moved = [filled] + [on_x(filled, k) for k in SHIFTS[1:]]
    block = jnp.stack(near)
    mine = [block] + [lax.ppermute(block, PLANE, along(False, k)) for k in SHIFTS[1:]]
    other = [to_core(v) for v in mine]
    terms = score(info, mine + other, moved)
    received = lax.all_to_all(terms, ("z", "yhi"), 0, 0, tiled=True)
    return place(received)


def solution(mesh):
    fine = Mesh(mesh.devices.reshape(SIZES), NAMES)
    corpus = ("z", "yhi", "x")
    query = ("ylo", "core")
    return jax.shard_map(
        per_device,
        mesh=fine,
        in_specs=(P(corpus, query, None), P(query + corpus, None, None), P(query + corpus)),
        out_specs=P(corpus, query),
        check_vma=False,
    )
```

```python
import functools

import jax
import jax.numpy as jnp
from jax import lax
from jax.experimental import pallas as pl
from jax.experimental.pallas import tpu as pltpu
from jax.sharding import Mesh
from jax.sharding import PartitionSpec as P

NAMES = ("ylo", "core", "z", "yhi", "x")
SIZES = (2, 2, 4, 2, 4)
PLANE = ("ylo", "core", "z", "yhi")
SHIFTS = (0, 1, -1, 2)
OWN, SLOTS, WIDTH = 8, 128, 128
DEPTH = 16
LOWEST = -3.0e38


def plane_pairs(move):
    def index(ylo, core, z, yhi):
        return ((ylo * 2 + core) * 4 + z) * 2 + yhi

    pairs = []
    for ylo in range(2):
        for core in range(2):
            for z in range(4):
                for yhi in range(2):
                    y2, core2, z2 = move(2 * yhi + ylo, core, z)
                    y2, z2 = y2 % 4, z2 % 4
                    pairs.append((index(ylo, core, z, yhi), index(y2 % 2, core2, z2, y2 // 2)))
    return pairs


def along(first, shift):
    def move(y, core, z):
        if (core == 0) == first:
            return y + shift, core, z
        return y, core, z + shift

    return plane_pairs(move)


def to_core(v):
    return lax.ppermute(v, "core", [(0, 1), (1, 0)])


def on_x(v, shift):
    pairs = [
        (core * 4 + i, core * 4 + (i + (shift if core == 0 else -shift)) % 4)
        for core in range(2)
        for i in range(4)
    ]
    return lax.ppermute(v, ("core", "x"), pairs)


def with_lengths(passages, lengths):
    tail = jnp.pad(lengths.astype(passages.dtype), (0, WIDTH - OWN))
    return jnp.concatenate(
        [passages.reshape(OWN * SLOTS, WIDTH), jnp.broadcast_to(tail, (16, WIDTH))], axis=0
    )


def best_dots(w_ref, p_ref, m_ref, s_ref, unit_ref, turns, *acc):
    acc = (acc[:DEPTH], acc[DEPTH:])
    nothing = jnp.zeros((16, 128), jnp.bfloat16)

    def push(g):
        for u in range(2):
            pltpu.matmul_push_rhs(w_ref[g * 2 + u], 0, u, transpose=True)

    def issue(unit, j, fresh=False):
        slots = p_ref[pl.ds(pl.multiple_of(unit, 16), 16), :]
        lhs = jnp.concatenate(
            [
                jnp.concatenate([slots, nothing], axis=1),
                jnp.concatenate([nothing, slots], axis=1),
            ],
            axis=0,
        )
        for u in range(2):
            pltpu.matmul_acc_lhs(acc[u][j], lhs, load_staged_rhs=0 if fresh else None)

    def take(unit, j):
        at = lax.shift_right_logical(unit, 7)
        begin = jnp.where(lax.bitwise_and(unit, 127) == 0, 32, at)
        tops = []
        held = [m_ref[b, begin] for b in range(8)]
        for u in range(2):
            d = pltpu.matmul_pop(acc[u][j])
            for half in range(2):
                top = jnp.maximum(d[16 * half : 16 * half + 8], d[16 * half + 8 : 16 * half + 16])
                tops += [top[:, 0:128], top[:, 128:256]]
        for b in range(8):
            m_ref[b, at] = jnp.maximum(held[b], tops[b])

    m_ref[:, 32] = jnp.full((8, 8, 128), LOWEST, jnp.float32)
    push(0)
    for j in range(DEPTH):
        issue(unit_ref[j], j, fresh=j == 0)

    def group(g, carry):
        push(jnp.minimum(g + 1, 7))

        def turn(t, c):
            for j in range(DEPTH):
                take(unit_ref[t * DEPTH + j], j)
                issue(unit_ref[t * DEPTH + DEPTH + j], j)
            return c

        lax.fori_loop(0, turns - 1, turn, 0)
        last = (turns - 1) * DEPTH
        for j in range(DEPTH):
            take(unit_ref[last + j], j)
            issue(unit_ref[j], j, fresh=j == 0)
        rows_ref = m_ref.reshape(8, 264, 128)
        for o in range(4):
            for side in range(2):
                total = None
                for b in range(side, 8, 2):
                    top = rows_ref[b, pl.ds(64 * o, 8, stride=8), :]
                    for i in range(1, 8):
                        top = jnp.maximum(top, rows_ref[b, pl.ds(64 * o + i, 8, stride=8), :])
                    total = top if total is None else total + top
                s_ref[g, 8 * o : 8 * o + 8, 128 * side : 128 * side + 128] = total
        return carry

    lax.fori_loop(0, 8, group, 0)
    for u in range(2):
        for j in range(DEPTH):
            m_ref[0, 0] = pltpu.matmul_pop(acc[u][j])[0:8, 0:128]


def score_kernel(info_ref, *refs):
    rows, pieces, out_ref = refs[:8], refs[8:12], refs[12]
    w_ref, p_ref, m_ref, s_ref, unit_ref = refs[13:]
    z, yhi, core, x, ylo = (info_ref[i] for i in range(5))
    mate = 2 - ylo

    for kind in range(2):

        @pl.when(core == kind)
        def _():
            for a in range(8):
                for j in range(4):
                    same = (a < 4) == (kind == 0)
                    dz, dy = (a % 4, j) if same else (j, a % 4)
                    h = {0: 0, 3: 1}.get(dy, (mate != dy).astype(jnp.int32))
                    half = 128 * (dy in (1, 2))
                    w_ref[(dz * 2 + h) * 2 + a // 4, :, half : half + 128] = rows[a][j]

    count = jnp.int32(0)
    for m in range(4):
        from_x = lax.rem(x + 4 - jnp.where(core == 0, SHIFTS[m], -SHIFTS[m]), 4)
        p_ref[pl.ds(pl.multiple_of(from_x * 1024, 1024), 1024), :] = pieces[m][0:1024, :]
        lengths = pieces[m][1024:1040, :].astype(jnp.float32)[0:8].astype(jnp.int32)
        units = lax.shift_right_logical(lengths + 15, 4)
        for i in range(OWN):
            for n in range(8):
                unit_ref[count + n] = from_x * 1024 + i * SLOTS + n * 16
            count = count + units[0, i]
            used = units[0, i]
            last = pl.multiple_of(from_x * 1024 + i * SLOTS + (used - 1) * 16, 16)
            both = p_ref[pl.ds(last, 16), :].astype(jnp.float32)
            second = jnp.where(lengths[0, i] == used * 16, both[8:16], both[0:8])
            p_ref[pl.ds(last, 16), :] = jnp.concatenate([both[0:8], second], axis=0).astype(p_ref.dtype)
    for i in range(DEPTH):
        unit_ref[count + i] = unit_ref[count - 1]
    turns = lax.div(count + DEPTH - 1, DEPTH)

    pl.run_scoped(
        functools.partial(best_dots, w_ref, p_ref, m_ref, s_ref, unit_ref, turns),
        *[pltpu.ACC(u)((32, 256), jnp.float32) for u in range(2) for _ in range(DEPTH)],
    )

    lane = lax.broadcasted_iota(jnp.int32, (32, 256), 1)
    row = lax.broadcasted_iota(jnp.int32, (32, 256), 0)
    pick = jnp.where(lane // 8 == row, 1.0 / 32, 0.0).astype(jnp.bfloat16)
    rest = s_ref[...].reshape(256, 256)
    parts = []
    for _ in range(3):
        parts.append(rest.astype(jnp.bfloat16))
        rest = rest - parts[-1].astype(jnp.float32)

    def add_up(acc):
        for part in parts:
            pltpu.matmul_push_rhs(part, 0, 0, transpose=True)
            pltpu.matmul_acc_lhs(acc, pick, load_staged_rhs=0)
        return pltpu.matmul_pop(acc)

    r = pl.run_scoped(add_up, pltpu.ACC(0)((32, 256), jnp.float32))
    for g in range(8):
        c = r[:, 32 * g : 32 * g + 32]
        place = lax.rem(z + 4 - SHIFTS[g // 2], 4) * 2 + (yhi if g % 2 == 0 else 1 - yhi)
        out_ref[place] = jnp.concatenate([c[0:8], c[8:16], c[16:24], c[24:32]], axis=1)


def score(info, rows, pieces):
    return pl.pallas_call(
        score_kernel,
        out_shape=jax.ShapeDtypeStruct((8, 8, 128), jnp.float32),
        in_specs=[pl.BlockSpec(memory_space=pltpu.SMEM)]
        + [pl.BlockSpec(memory_space=pltpu.VMEM)] * 12,
        out_specs=pl.BlockSpec(memory_space=pltpu.VMEM),
        scratch_shapes=[
            pltpu.VMEM((16, 256, 256), jnp.bfloat16),
            pltpu.VMEM((4096, 128), jnp.bfloat16),
            pltpu.VMEM((8, 33, 8, 128), jnp.float32),
            pltpu.VMEM((8, 32, 256), jnp.float32),
            pltpu.SMEM((256 + DEPTH,), jnp.int32),
        ],
        compiler_params=pltpu.CompilerParams(vmem_limit_bytes=32 << 20),
    )(info, *rows, *pieces)


def place_kernel(r_ref, o_ref):
    for g in range(4):
        o_ref[8 * g : 8 * g + 8, :] = jnp.concatenate(
            [r_ref[s][:, 32 * g : 32 * g + 32] for s in range(8)], axis=1
        )


def place(received):
    return pl.pallas_call(
        place_kernel,
        out_shape=jax.ShapeDtypeStruct((32, 256), jnp.float32),
        in_specs=[pl.BlockSpec(memory_space=pltpu.VMEM)],
        out_specs=pl.BlockSpec(memory_space=pltpu.VMEM),
    )(received)


def per_device(queries, passages, lengths):
    own = queries.reshape(256, 128)
    info = jnp.stack([lax.axis_index(name) for name in ("z", "yhi", "core", "x", "ylo")]).astype(jnp.int32)

    near = [own] + [lax.ppermute(own, PLANE, along(True, k)) for k in SHIFTS[1:]]
    filled = with_lengths(passages, lengths)
    once = on_x(filled, 1)
    moved = [filled, once, on_x(filled, -1), on_x(once, 1)]
    block = jnp.stack(near)
    mine = [block] + [lax.ppermute(block, PLANE, along(False, k)) for k in SHIFTS[1:]]
    other = [to_core(v) for v in mine]
    terms = score(info, mine + other, moved)
    received = lax.all_to_all(terms, ("z", "yhi"), 0, 0, tiled=True)
    return place(received)


def solution(mesh):
    fine = Mesh(mesh.devices.reshape(SIZES), NAMES)
    corpus = ("z", "yhi", "x")
    query = ("ylo", "core")
    return jax.shard_map(
        per_device,
        mesh=fine,
        in_specs=(P(corpus, query, None), P(query + corpus, None, None), P(query + corpus)),
        out_specs=P(corpus, query),
        check_vma=False,
    )
```

```python
import functools

import jax
import jax.numpy as jnp
from jax import lax
from jax.experimental import pallas as pl
from jax.experimental.pallas import tpu as pltpu
from jax.sharding import Mesh
from jax.sharding import PartitionSpec as P

NAMES = ("ylo", "core", "z", "yhi", "x")
SIZES = (2, 2, 4, 2, 4)
PLANE = ("ylo", "core", "z", "yhi")
SHIFTS = (0, 1, -1, 2)
OWN, SLOTS, WIDTH = 8, 128, 128
DEPTH = 16
LOWEST = -3.0e38
UNITS = 384


def plane_pairs(move):
    def index(ylo, core, z, yhi):
        return ((ylo * 2 + core) * 4 + z) * 2 + yhi

    pairs = []
    for ylo in range(2):
        for core in range(2):
            for z in range(4):
                for yhi in range(2):
                    y2, core2, z2 = move(2 * yhi + ylo, core, z)
                    y2, z2 = y2 % 4, z2 % 4
                    pairs.append((index(ylo, core, z, yhi), index(y2 % 2, core2, z2, y2 // 2)))
    return pairs


def along(first, shift):
    def move(y, core, z):
        if (core == 0) == first:
            return y + shift, core, z
        return y, core, z + shift

    return plane_pairs(move)


def to_core(v):
    return lax.ppermute(v, "core", [(0, 1), (1, 0)])


def on_x(v, shift):
    pairs = [
        (core * 4 + i, core * 4 + (i + (shift if core == 0 else -shift)) % 4)
        for core in range(2)
        for i in range(4)
    ]
    return lax.ppermute(v, ("core", "x"), pairs)


def with_lengths(passages, lengths):
    tail = jnp.pad(lengths.astype(passages.dtype), (0, WIDTH - OWN))
    return jnp.concatenate(
        [passages.reshape(OWN * SLOTS, WIDTH), jnp.broadcast_to(tail, (16, WIDTH))], axis=0
    )


def prepare_kernel(info_ref, *refs):
    pieces, p_ref, unit_ref = refs[:4], refs[4], refs[5]
    core, x = info_ref[2], info_ref[3]
    count = jnp.int32(0)
    for m in range(4):
        from_x = lax.rem(x + 4 - jnp.where(core == 0, SHIFTS[m], -SHIFTS[m]), 4)
        p_ref[pl.ds(pl.multiple_of(from_x * 1024, 1024), 1024), :] = pieces[m][0:1024, :]
        lengths = pieces[m][1024:1040, :].astype(jnp.float32)[0:8].astype(jnp.int32)
        units = lax.shift_right_logical(lengths + 15, 4)
        for i in range(OWN):
            for n in range(8):
                unit_ref[count + n] = from_x * 1024 + i * SLOTS + n * 16
            count = count + units[0, i]
            used = units[0, i]
            last = pl.multiple_of(from_x * 1024 + i * SLOTS + (used - 1) * 16, 16)
            both = p_ref[pl.ds(last, 16), :].astype(jnp.float32)
            second = jnp.where(lengths[0, i] == used * 16, both[8:16], both[0:8])
            p_ref[pl.ds(last, 16), :] = jnp.concatenate([both[0:8], second], axis=0).astype(p_ref.dtype)
    for i in range(DEPTH):
        unit_ref[count + i] = unit_ref[count - 1]
    unit_ref[UNITS - 1] = lax.div(count + DEPTH - 1, DEPTH)


def prepare(info, pieces):
    return pl.pallas_call(
        prepare_kernel,
        out_shape=[
            jax.ShapeDtypeStruct((4096, WIDTH), jnp.bfloat16),
            jax.ShapeDtypeStruct((UNITS,), jnp.int32),
        ],
        in_specs=[pl.BlockSpec(memory_space=pltpu.SMEM)]
        + [pl.BlockSpec(memory_space=pltpu.VMEM)] * 4,
        out_specs=[pl.BlockSpec(memory_space=pltpu.VMEM), pl.BlockSpec(memory_space=pltpu.SMEM)],
        compiler_params=pltpu.CompilerParams(vmem_limit_bytes=16 << 20),
        cost_estimate=pl.CostEstimate(flops=1 << 30, bytes_accessed=2 << 20, transcendentals=0),
    )(info, *pieces)


def best_dots(rows, places, p_ref, m_ref, s_ref, unit_ref, turns, *acc):
    acc = (acc[:DEPTH], acc[DEPTH:])
    nothing = jnp.zeros((16, 128), jnp.bfloat16)

    def push(g):
        for u in range(2):
            held = jnp.concatenate([ref[j] for ref, j in rows[g][2 * u : 2 * u + 2]], axis=1)
            pltpu.matmul_push_rhs(held, 0, u, transpose=True)

    def issue(unit, j, fresh=False):
        slots = p_ref[pl.ds(pl.multiple_of(unit, 16), 16), :]
        lhs = jnp.concatenate(
            [
                jnp.concatenate([slots, nothing], axis=1),
                jnp.concatenate([nothing, slots], axis=1),
            ],
            axis=0,
        )
        for u in range(2):
            pltpu.matmul_acc_lhs(acc[u][j], lhs, load_staged_rhs=0 if fresh else None)

    def take(unit, j):
        at = lax.shift_right_logical(unit, 7)
        begin = jnp.where(lax.bitwise_and(unit, 127) == 0, 32, at)
        tops = []
        held = [m_ref[b, begin] for b in range(8)]
        for u in range(2):
            d = pltpu.matmul_pop(acc[u][j])
            for half in range(2):
                top = jnp.maximum(d[16 * half : 16 * half + 8], d[16 * half + 8 : 16 * half + 16])
                tops += [top[:, 0:128], top[:, 128:256]]
        for b in range(8):
            m_ref[b, at] = jnp.maximum(held[b], tops[b])

    def turn(t, c):
        for j in range(DEPTH):
            take(unit_ref[t * DEPTH + j], j)
            issue(unit_ref[t * DEPTH + DEPTH + j], j)
        return c

    m_ref[:, 32] = jnp.full((8, 8, 128), LOWEST, jnp.float32)
    rows_ref = m_ref.reshape(8, 264, 128)
    push(0)
    for j in range(DEPTH):
        issue(unit_ref[j], j, fresh=j == 0)
    for g in range(len(rows)):
        lax.fori_loop(0, turns - 1, turn, 0)
        more = g + 1 < len(rows)
        if more:
            push(g + 1)
        last = (turns - 1) * DEPTH
        for j in range(DEPTH):
            take(unit_ref[last + j], j)
            if more:
                issue(unit_ref[j], j, fresh=j == 0)
        for o in range(4):
            for b in range(8):
                top = rows_ref[b, pl.ds(64 * o, 8, stride=8), :]
                for i in range(1, 8):
                    top = jnp.maximum(top, rows_ref[b, pl.ds(64 * o + i, 8, stride=8), :])
                lanes = slice(128 * (b % 2), 128 * (b % 2) + 128)
                s_ref[places[g][b // 2], 8 * o : 8 * o + 8, lanes] += top


def score_kernel(shifts, parts, info_ref, unit_ref, p_ref, *refs):
    n = 2 * len(shifts)
    rows, sums, out_ref, m_ref = refs[:n], refs[n : n + parts], refs[n + parts], refs[n + parts + 1]
    s_ref = refs[n + parts + 2] if parts else out_ref
    z, yhi, core, ylo = info_ref[0], info_ref[1], info_ref[2], info_ref[4]
    y = yhi * 2 + ylo

    def place(chain, k, j):
        from_z = lax.rem(z + 4 - jnp.where(chain == 0, SHIFTS[k], SHIFTS[j]), 4)
        from_y = lax.rem(y + 4 - jnp.where(chain == 0, SHIFTS[j], SHIFTS[k]), 4)
        return from_z * 2 + lax.shift_right_logical(from_y, 1)

    groups, places = [], []
    for i, k in enumerate(shifts):
        mine, other = rows[2 * i], rows[2 * i + 1]
        for j in (0, 2):
            groups.append([(mine, j), (mine, j + 1), (other, j), (other, j + 1)])
            places.append([place(chain, k, j + e) for chain in (core, 1 - core) for e in range(2)])
    total = jnp.zeros(s_ref.shape, jnp.float32)
    for part in sums:
        total = total + part[...]
    s_ref[...] = total
    pl.run_scoped(
        functools.partial(best_dots, groups, places, p_ref, m_ref, s_ref, unit_ref, unit_ref[UNITS - 1]),
        *[pltpu.ACC(u)((32, 256), jnp.float32) for u in range(2) for _ in range(DEPTH)],
    )
    if not parts:
        return

    lane = lax.broadcasted_iota(jnp.int32, (32, 256), 1)
    row = lax.broadcasted_iota(jnp.int32, (32, 256), 0)
    pick = jnp.where(lane // 8 == row, 1.0 / 32, 0.0).astype(jnp.bfloat16)
    rest = s_ref[...].reshape(256, 256)
    split = []
    for _ in range(3):
        split.append(rest.astype(jnp.bfloat16))
        rest = rest - split[-1].astype(jnp.float32)

    def add_up(acc):
        for part in split:
            pltpu.matmul_push_rhs(part, 0, 0, transpose=True)
            pltpu.matmul_acc_lhs(acc, pick, load_staged_rhs=0)
        return pltpu.matmul_pop(acc)

    r = pl.run_scoped(add_up, pltpu.ACC(0)((32, 256), jnp.float32))
    for g in range(8):
        c = r[:, 32 * g : 32 * g + 32]
        out_ref[g] = jnp.concatenate([c[0:8], c[8:16], c[16:24], c[24:32]], axis=1)


def score(info, units, slots, shifts, rows, sums=()):
    sums_shape = (8, 32, 256)
    return pl.pallas_call(
        functools.partial(score_kernel, shifts, len(sums)),
        out_shape=jax.ShapeDtypeStruct((8, 8, 128) if sums else sums_shape, jnp.float32),
        in_specs=[pl.BlockSpec(memory_space=pltpu.SMEM)] * 2
        + [pl.BlockSpec(memory_space=pltpu.VMEM)] * (1 + len(rows) + len(sums)),
        out_specs=pl.BlockSpec(memory_space=pltpu.VMEM),
        scratch_shapes=[pltpu.VMEM((8, 33, 8, 128), jnp.float32)]
        + ([pltpu.VMEM(sums_shape, jnp.float32)] if sums else []),
        compiler_params=pltpu.CompilerParams(vmem_limit_bytes=32 << 20),
        cost_estimate=pl.CostEstimate(
            flops=len(shifts) * 2048 * 4096 * 256 * 2, bytes_accessed=2 << 20, transcendentals=0
        ),
    )(info, units, slots, *rows, *sums)


def place_kernel(r_ref, o_ref):
    for g in range(4):
        o_ref[8 * g : 8 * g + 8, :] = jnp.concatenate(
            [r_ref[s][:, 32 * g : 32 * g + 32] for s in range(8)], axis=1
        )


def place(received):
    return pl.pallas_call(
        place_kernel,
        out_shape=jax.ShapeDtypeStruct((32, 256), jnp.float32),
        in_specs=[pl.BlockSpec(memory_space=pltpu.VMEM)],
        out_specs=pl.BlockSpec(memory_space=pltpu.VMEM),
    )(received)


def per_device(queries, passages, lengths):
    own = queries.reshape(256, 128)
    info = jnp.stack([lax.axis_index(name) for name in ("z", "yhi", "core", "x", "ylo")]).astype(jnp.int32)

    near = [own] + [lax.ppermute(own, PLANE, along(True, k)) for k in SHIFTS[1:]]
    filled = with_lengths(passages, lengths)
    once = on_x(filled, 1)
    moved = [filled, once, on_x(filled, -1), on_x(once, 1)]
    block = jnp.stack(near)
    slots, units = prepare(info, moved)
    mine = [block] + [lax.ppermute(block, PLANE, along(False, k)) for k in SHIFTS[1:]]
    first = score(info, units, slots, (0,), (block, to_core(block)))
    first, *late = lax.optimization_barrier((first, *mine[1:]))
    rows = [w for v in late for w in (v, to_core(v))]
    terms = score(info, units, slots, (1, 2, 3), rows, (first,))
    received = lax.all_to_all(terms, ("z", "yhi"), 0, 0, tiled=True)
    return place(received)


def solution(mesh):
    fine = Mesh(mesh.devices.reshape(SIZES), NAMES)
    corpus = ("z", "yhi", "x")
    query = ("ylo", "core")
    return jax.shard_map(
        per_device,
        mesh=fine,
        in_specs=(P(corpus, query, None), P(query + corpus, None, None), P(query + corpus)),
        out_specs=P(corpus, query),
        check_vma=False,
    )
```

```python
import functools

import jax
import jax.numpy as jnp
from jax import lax
from jax.experimental import pallas as pl
from jax.experimental.pallas import tpu as pltpu
from jax.sharding import Mesh
from jax.sharding import PartitionSpec as P

NAMES = ("ylo", "core", "z", "yhi", "x")
SIZES = (2, 2, 4, 2, 4)
PLANE = ("ylo", "core", "z", "yhi")
SHIFTS = (0, 1, -1, 2)
OWN, SLOTS, WIDTH = 8, 128, 128
DEPTH = 16
LOWEST = -3.0e38
UNITS = 384


def plane_pairs(move):
    def index(ylo, core, z, yhi):
        return ((ylo * 2 + core) * 4 + z) * 2 + yhi

    pairs = []
    for ylo in range(2):
        for core in range(2):
            for z in range(4):
                for yhi in range(2):
                    y2, core2, z2 = move(2 * yhi + ylo, core, z)
                    y2, z2 = y2 % 4, z2 % 4
                    pairs.append((index(ylo, core, z, yhi), index(y2 % 2, core2, z2, y2 // 2)))
    return pairs


def along(first, shift):
    def move(y, core, z):
        if (core == 0) == first:
            return y + shift, core, z
        return y, core, z + shift

    return plane_pairs(move)


def to_core(v):
    return lax.ppermute(v, "core", [(0, 1), (1, 0)])


def on_x(v, shift):
    pairs = [
        (core * 4 + i, core * 4 + (i + (shift if core == 0 else -shift)) % 4)
        for core in range(2)
        for i in range(4)
    ]
    return lax.ppermute(v, ("core", "x"), pairs)


def with_lengths(passages, lengths):
    tail = jnp.pad(lengths.astype(passages.dtype), (0, WIDTH - OWN))
    return jnp.concatenate(
        [passages.reshape(OWN * SLOTS, WIDTH), jnp.broadcast_to(tail, (16, WIDTH))], axis=0
    )


def prepare(core, x, pieces, p_ref, unit_ref):
    count = jnp.int32(0)
    for m in range(4):
        from_x = lax.rem(x + 4 - jnp.where(core == 0, SHIFTS[m], -SHIFTS[m]), 4)
        p_ref[pl.ds(pl.multiple_of(from_x * 1024, 1024), 1024), :] = pieces[m][0:1024, :]
        lengths = pieces[m][1024:1040, :].astype(jnp.float32)[0:8].astype(jnp.int32)
        units = lax.shift_right_logical(lengths + 15, 4)
        for i in range(OWN):
            for n in range(8):
                unit_ref[count + n] = from_x * 1024 + i * SLOTS + n * 16
            count = count + units[0, i]
            used = units[0, i]
            last = pl.multiple_of(from_x * 1024 + i * SLOTS + (used - 1) * 16, 16)
            both = p_ref[pl.ds(last, 16), :].astype(jnp.float32)
            second = jnp.where(lengths[0, i] == used * 16, both[8:16], both[0:8])
            p_ref[pl.ds(last, 16), :] = jnp.concatenate([both[0:8], second], axis=0).astype(p_ref.dtype)
    for i in range(DEPTH):
        unit_ref[count + i] = unit_ref[count - 1]
    unit_ref[UNITS - 1] = lax.div(count + DEPTH - 1, DEPTH)


def best_dots(rows, places, p_ref, m_ref, s_ref, unit_ref, turns, *acc):
    acc = (acc[:DEPTH], acc[DEPTH:])
    nothing = jnp.zeros((16, 128), jnp.bfloat16)

    def push(g):
        for u in range(2):
            held = jnp.concatenate([ref[j] for ref, j in rows[g][2 * u : 2 * u + 2]], axis=1)
            pltpu.matmul_push_rhs(held, 0, u, transpose=True)

    def issue(unit, j, fresh=False):
        slots = p_ref[pl.ds(pl.multiple_of(unit, 16), 16), :]
        lhs = jnp.concatenate(
            [
                jnp.concatenate([slots, nothing], axis=1),
                jnp.concatenate([nothing, slots], axis=1),
            ],
            axis=0,
        )
        for u in range(2):
            pltpu.matmul_acc_lhs(acc[u][j], lhs, load_staged_rhs=0 if fresh else None)

    def take(unit, j):
        at = lax.shift_right_logical(unit, 7)
        begin = jnp.where(lax.bitwise_and(unit, 127) == 0, 32, at)
        tops = []
        held = [m_ref[b, begin] for b in range(8)]
        for u in range(2):
            d = pltpu.matmul_pop(acc[u][j])
            for half in range(2):
                top = jnp.maximum(d[16 * half : 16 * half + 8], d[16 * half + 8 : 16 * half + 16])
                tops += [top[:, 0:128], top[:, 128:256]]
        for b in range(8):
            m_ref[b, at] = jnp.maximum(held[b], tops[b])

    def turn(t, c):
        for j in range(DEPTH):
            take(unit_ref[t * DEPTH + j], j)
            issue(unit_ref[t * DEPTH + DEPTH + j], j)
        return c

    m_ref[:, 32] = jnp.full((8, 8, 128), LOWEST, jnp.float32)
    rows_ref = m_ref.reshape(8, 264, 128)
    push(0)
    for j in range(DEPTH):
        issue(unit_ref[j], j, fresh=j == 0)
    for g in range(len(rows)):
        lax.fori_loop(0, turns - 1, turn, 0)
        more = g + 1 < len(rows)
        if more:
            push(g + 1)
        last = (turns - 1) * DEPTH
        for j in range(DEPTH):
            take(unit_ref[last + j], j)
            if more:
                issue(unit_ref[j], j, fresh=j == 0)
        for o in range(4):
            for b in range(8):
                top = rows_ref[b, pl.ds(64 * o, 8, stride=8), :]
                for i in range(1, 8):
                    top = jnp.maximum(top, rows_ref[b, pl.ds(64 * o + i, 8, stride=8), :])
                lanes = slice(128 * (b % 2), 128 * (b % 2) + 128)
                s_ref[places[g][b // 2], 8 * o : 8 * o + 8, lanes] += top


def first_kernel(info_ref, *refs):
    pieces, rows, (p_ref, unit_ref, s_ref, m_ref) = refs[:4], refs[4:6], refs[6:]
    prepare(info_ref[2], info_ref[3], pieces, p_ref, unit_ref)
    s_ref[...] = jnp.zeros_like(s_ref)
    score_rows(info_ref, unit_ref, p_ref, (0,), rows, s_ref, m_ref)


def last_kernel(shifts, info_ref, unit_ref, p_ref, *refs):
    n = 2 * len(shifts)
    rows, (sum_ref, out_ref, s_ref, m_ref) = refs[:n], refs[n:]
    s_ref[...] = sum_ref[...]
    score_rows(info_ref, unit_ref, p_ref, shifts, rows, s_ref, m_ref)
    pack(s_ref, out_ref)


def score_rows(info_ref, unit_ref, p_ref, shifts, rows, s_ref, m_ref):
    z, yhi, core, ylo = info_ref[0], info_ref[1], info_ref[2], info_ref[4]
    y = yhi * 2 + ylo

    def place(chain, k, j):
        from_z = lax.rem(z + 4 - jnp.where(chain == 0, SHIFTS[k], SHIFTS[j]), 4)
        from_y = lax.rem(y + 4 - jnp.where(chain == 0, SHIFTS[j], SHIFTS[k]), 4)
        return from_z * 2 + lax.shift_right_logical(from_y, 1)

    groups, places = [], []
    for i, k in enumerate(shifts):
        mine, other = rows[2 * i], rows[2 * i + 1]
        for j in (0, 2):
            groups.append([(mine, j), (mine, j + 1), (other, j), (other, j + 1)])
            places.append([place(chain, k, j + e) for chain in (core, 1 - core) for e in range(2)])
    pl.run_scoped(
        functools.partial(best_dots, groups, places, p_ref, m_ref, s_ref, unit_ref, unit_ref[UNITS - 1]),
        *[pltpu.ACC(u)((32, 256), jnp.float32) for u in range(2) for _ in range(DEPTH)],
    )


def pack(s_ref, out_ref):
    lane = lax.broadcasted_iota(jnp.int32, (32, 256), 1)
    row = lax.broadcasted_iota(jnp.int32, (32, 256), 0)
    pick = jnp.where(lane // 8 == row, 1.0 / 32, 0.0).astype(jnp.bfloat16)
    rest = s_ref[...].reshape(256, 256)
    split = []
    for _ in range(3):
        split.append(rest.astype(jnp.bfloat16))
        rest = rest - split[-1].astype(jnp.float32)

    def add_up(acc):
        for part in split:
            pltpu.matmul_push_rhs(part, 0, 0, transpose=True)
            pltpu.matmul_acc_lhs(acc, pick, load_staged_rhs=0)
        return pltpu.matmul_pop(acc)

    r = pl.run_scoped(add_up, pltpu.ACC(0)((32, 256), jnp.float32))
    for g in range(8):
        c = r[:, 32 * g : 32 * g + 32]
        out_ref[g] = jnp.concatenate([c[0:8], c[8:16], c[16:24], c[24:32]], axis=1)


SUMS = (8, 32, 256)


def cost(arrays):
    return pl.CostEstimate(
        flops=arrays * 2048 * 4096 * 256 * 2, bytes_accessed=2 << 20, transcendentals=0
    )


def score_first(info, pieces, rows):
    return pl.pallas_call(
        first_kernel,
        out_shape=[
            jax.ShapeDtypeStruct((4096, WIDTH), jnp.bfloat16),
            jax.ShapeDtypeStruct((UNITS,), jnp.int32),
            jax.ShapeDtypeStruct(SUMS, jnp.float32),
        ],
        in_specs=[pl.BlockSpec(memory_space=pltpu.SMEM)]
        + [pl.BlockSpec(memory_space=pltpu.VMEM)] * 6,
        out_specs=[
            pl.BlockSpec(memory_space=pltpu.VMEM),
            pl.BlockSpec(memory_space=pltpu.SMEM),
            pl.BlockSpec(memory_space=pltpu.VMEM),
        ],
        scratch_shapes=[pltpu.VMEM((8, 33, 8, 128), jnp.float32)],
        compiler_params=pltpu.CompilerParams(vmem_limit_bytes=32 << 20),
        cost_estimate=cost(1),
    )(info, *pieces, *rows)


def score_last(info, units, slots, shifts, rows, sums):
    return pl.pallas_call(
        functools.partial(last_kernel, shifts),
        out_shape=jax.ShapeDtypeStruct((8, 8, 128), jnp.float32),
        in_specs=[pl.BlockSpec(memory_space=pltpu.SMEM)] * 2
        + [pl.BlockSpec(memory_space=pltpu.VMEM)] * (2 + len(rows)),
        out_specs=pl.BlockSpec(memory_space=pltpu.VMEM),
        scratch_shapes=[pltpu.VMEM(SUMS, jnp.float32), pltpu.VMEM((8, 33, 8, 128), jnp.float32)],
        compiler_params=pltpu.CompilerParams(vmem_limit_bytes=32 << 20),
        cost_estimate=cost(len(shifts)),
    )(info, units, slots, *rows, sums)


def place_kernel(r_ref, o_ref):
    for g in range(4):
        o_ref[8 * g : 8 * g + 8, :] = jnp.concatenate(
            [r_ref[s][:, 32 * g : 32 * g + 32] for s in range(8)], axis=1
        )


def place(received):
    return pl.pallas_call(
        place_kernel,
        out_shape=jax.ShapeDtypeStruct((32, 256), jnp.float32),
        in_specs=[pl.BlockSpec(memory_space=pltpu.VMEM)],
        out_specs=pl.BlockSpec(memory_space=pltpu.VMEM),
    )(received)


def per_device(queries, passages, lengths):
    own = queries.reshape(256, 128)
    info = jnp.stack([lax.axis_index(name) for name in ("z", "yhi", "core", "x", "ylo")]).astype(jnp.int32)

    near = [own] + [lax.ppermute(own, PLANE, along(True, k)) for k in SHIFTS[1:]]
    filled = with_lengths(passages, lengths)
    moved = [filled] + [on_x(filled, k) for k in SHIFTS[1:]]
    block = jnp.stack(near)
    mine = [lax.ppermute(block, PLANE, along(False, k)) for k in SHIFTS[1:]]
    slots, units, sums = score_first(info, moved, (block, to_core(block)))
    sums, mine[0] = lax.optimization_barrier((sums, mine[0]))
    rows = [w for v in mine for w in (v, to_core(v))]
    terms = score_last(info, units, slots, (1, 2, 3), rows, sums)
    received = lax.all_to_all(terms, ("z", "yhi"), 0, 0, tiled=True)
    return place(received)


def solution(mesh):
    fine = Mesh(mesh.devices.reshape(SIZES), NAMES)
    corpus = ("z", "yhi", "x")
    query = ("ylo", "core")
    return jax.shard_map(
        per_device,
        mesh=fine,
        in_specs=(P(corpus, query, None), P(query + corpus, None, None), P(query + corpus)),
        out_specs=P(corpus, query),
        check_vma=False,
    )
```

```python
import functools

import jax
import jax.numpy as jnp
from jax import lax
from jax.experimental import pallas as pl
from jax.experimental.pallas import tpu as pltpu
from jax.sharding import Mesh
from jax.sharding import PartitionSpec as P

NAMES = ("ylo", "core", "z", "yhi", "x")
SIZES = (2, 2, 4, 2, 4)
PLANE = ("ylo", "core", "z", "yhi")
SHIFTS = (0, 1, -1, 2)
OWN, SLOTS, WIDTH = 8, 128, 128
DEPTH = 16
LOWEST = -3.0e38
UNITS = 384


def plane_pairs(move):
    def index(ylo, core, z, yhi):
        return ((ylo * 2 + core) * 4 + z) * 2 + yhi

    pairs = []
    for ylo in range(2):
        for core in range(2):
            for z in range(4):
                for yhi in range(2):
                    y2, core2, z2 = move(2 * yhi + ylo, core, z)
                    y2, z2 = y2 % 4, z2 % 4
                    pairs.append((index(ylo, core, z, yhi), index(y2 % 2, core2, z2, y2 // 2)))
    return pairs


def along(first, shift):
    def move(y, core, z):
        if (core == 0) == first:
            return y + shift, core, z
        return y, core, z + shift

    return plane_pairs(move)


def to_core(v):
    return lax.ppermute(v, "core", [(0, 1), (1, 0)])


def on_x(v, shift):
    pairs = [
        (core * 4 + i, core * 4 + (i + (shift if core == 0 else -shift)) % 4)
        for core in range(2)
        for i in range(4)
    ]
    return lax.ppermute(v, ("core", "x"), pairs)


def with_lengths(passages, lengths):
    tail = jnp.pad(lengths.astype(passages.dtype), (0, WIDTH - OWN))
    return jnp.concatenate(
        [passages.reshape(OWN * SLOTS, WIDTH), jnp.broadcast_to(tail, (16, WIDTH))], axis=0
    )


def prepare(core, x, pieces, p_ref, unit_ref):
    count = jnp.int32(0)
    for m in range(4):
        from_x = lax.rem(x + 4 - jnp.where(core == 0, SHIFTS[m], -SHIFTS[m]), 4)
        p_ref[pl.ds(pl.multiple_of(from_x * 1024, 1024), 1024), :] = pieces[m][0:1024, :]
        lengths = pieces[m][1024:1040, :].astype(jnp.float32)[0:8].astype(jnp.int32)
        units = lax.shift_right_logical(lengths + 15, 4)
        for i in range(OWN):
            for n in range(8):
                unit_ref[count + n] = from_x * 1024 + i * SLOTS + n * 16
            count = count + units[0, i]
            used = units[0, i]
            last = pl.multiple_of(from_x * 1024 + i * SLOTS + (used - 1) * 16, 16)
            both = p_ref[pl.ds(last, 16), :].astype(jnp.float32)
            second = jnp.where(lengths[0, i] == used * 16, both[8:16], both[0:8])
            p_ref[pl.ds(last, 16), :] = jnp.concatenate([both[0:8], second], axis=0).astype(p_ref.dtype)
    for i in range(DEPTH):
        unit_ref[count + i] = unit_ref[count - 1]
    unit_ref[UNITS - 1] = lax.div(count + DEPTH - 1, DEPTH)


def best_dots(rows, places, p_ref, m_ref, s_ref, unit_ref, turns, *acc):
    acc = (acc[:DEPTH], acc[DEPTH:])
    nothing = jnp.zeros((16, 128), jnp.bfloat16)

    def push(g):
        for u in range(2):
            held = jnp.concatenate([ref[j] for ref, j in rows[g][2 * u : 2 * u + 2]], axis=1)
            pltpu.matmul_push_rhs(held, 0, u, transpose=True)

    def issue(unit, j, fresh=False):
        slots = p_ref[pl.ds(pl.multiple_of(unit, 16), 16), :]
        lhs = jnp.concatenate(
            [
                jnp.concatenate([slots, nothing], axis=1),
                jnp.concatenate([nothing, slots], axis=1),
            ],
            axis=0,
        )
        for u in range(2):
            pltpu.matmul_acc_lhs(acc[u][j], lhs, load_staged_rhs=0 if fresh else None)

    def take(unit, j):
        at = lax.shift_right_logical(unit, 7)
        begin = jnp.where(lax.bitwise_and(unit, 127) == 0, 32, at)
        tops = []
        held = [m_ref[b, begin] for b in range(8)]
        for u in range(2):
            d = pltpu.matmul_pop(acc[u][j])
            for half in range(2):
                top = jnp.maximum(d[16 * half : 16 * half + 8], d[16 * half + 8 : 16 * half + 16])
                tops += [top[:, 0:128], top[:, 128:256]]
        for b in range(8):
            m_ref[b, at] = jnp.maximum(held[b], tops[b])

    def turn(t, c):
        for j in range(DEPTH):
            take(unit_ref[t * DEPTH + j], j)
            issue(unit_ref[t * DEPTH + DEPTH + j], j)
        return c

    m_ref[:, 32] = jnp.full((8, 8, 128), LOWEST, jnp.float32)
    rows_ref = m_ref.reshape(8, 264, 128)
    push(0)
    for j in range(DEPTH):
        issue(unit_ref[j], j, fresh=j == 0)
    for g in range(len(rows)):
        lax.fori_loop(0, turns - 1, turn, 0)
        more = g + 1 < len(rows)
        if more:
            push(g + 1)
        last = (turns - 1) * DEPTH
        for j in range(DEPTH):
            take(unit_ref[last + j], j)
            if more:
                issue(unit_ref[j], j, fresh=j == 0)
        for o in range(4):
            for b in range(8):
                top = rows_ref[b, pl.ds(64 * o, 8, stride=8), :]
                for i in range(1, 8):
                    top = jnp.maximum(top, rows_ref[b, pl.ds(64 * o + i, 8, stride=8), :])
                lanes = slice(128 * (b % 2), 128 * (b % 2) + 128)
                s_ref[places[g][b // 2], 8 * o : 8 * o + 8, lanes] += top


def first_kernel(info_ref, *refs):
    pieces, rows, (p_ref, unit_ref, s_ref, m_ref) = refs[:4], refs[4:6], refs[6:]
    prepare(info_ref[2], info_ref[3], pieces, p_ref, unit_ref)
    s_ref[...] = jnp.zeros_like(s_ref)
    score_rows(info_ref, unit_ref, p_ref, (0,), rows, s_ref, m_ref)


def last_kernel(shifts, info_ref, unit_ref, p_ref, *refs):
    n = 2 * len(shifts)
    rows, (sum_ref, out_ref, s_ref, m_ref) = refs[:n], refs[n:]
    s_ref[...] = sum_ref[...]
    score_rows(info_ref, unit_ref, p_ref, shifts, rows, s_ref, m_ref)
    pack(s_ref, out_ref)


def score_rows(info_ref, unit_ref, p_ref, shifts, rows, s_ref, m_ref):
    z, yhi, core, ylo = info_ref[0], info_ref[1], info_ref[2], info_ref[4]
    y = yhi * 2 + ylo

    def place(chain, k, j):
        from_z = lax.rem(z + 4 - jnp.where(chain == 0, SHIFTS[k], SHIFTS[j]), 4)
        from_y = lax.rem(y + 4 - jnp.where(chain == 0, SHIFTS[j], SHIFTS[k]), 4)
        return from_z * 2 + lax.shift_right_logical(from_y, 1)

    groups, places = [], []
    for i, k in enumerate(shifts):
        mine, other = rows[2 * i], rows[2 * i + 1]
        for j in (0, 2):
            groups.append([(mine, j), (mine, j + 1), (other, j), (other, j + 1)])
            places.append([place(chain, k, j + e) for chain in (core, 1 - core) for e in range(2)])
    pl.run_scoped(
        functools.partial(best_dots, groups, places, p_ref, m_ref, s_ref, unit_ref, unit_ref[UNITS - 1]),
        *[pltpu.ACC(u)((32, 256), jnp.float32) for u in range(2) for _ in range(DEPTH)],
    )


def pack(s_ref, out_ref):
    lane = lax.broadcasted_iota(jnp.int32, (32, 256), 1)
    row = lax.broadcasted_iota(jnp.int32, (32, 256), 0)
    pick = jnp.where(lane // 8 == row, 1.0 / 32, 0.0).astype(jnp.bfloat16)
    rest = s_ref[...].reshape(256, 256)
    split = []
    for _ in range(3):
        split.append(rest.astype(jnp.bfloat16))
        rest = rest - split[-1].astype(jnp.float32)

    def add_up(acc):
        for part in split:
            pltpu.matmul_push_rhs(part, 0, 0, transpose=True)
            pltpu.matmul_acc_lhs(acc, pick, load_staged_rhs=0)
        return pltpu.matmul_pop(acc)

    r = pl.run_scoped(add_up, pltpu.ACC(0)((32, 256), jnp.float32))
    for g in range(8):
        c = r[:, 32 * g : 32 * g + 32]
        out_ref[g] = jnp.concatenate([c[0:8], c[8:16], c[16:24], c[24:32]], axis=1)


SUMS = (8, 32, 256)


def cost(arrays):
    return pl.CostEstimate(
        flops=arrays * 2048 * 4096 * 256 * 2, bytes_accessed=2 << 20, transcendentals=0
    )


def score_first(info, pieces, rows):
    return pl.pallas_call(
        first_kernel,
        out_shape=[
            jax.ShapeDtypeStruct((4096, WIDTH), jnp.bfloat16),
            jax.ShapeDtypeStruct((UNITS,), jnp.int32),
            jax.ShapeDtypeStruct(SUMS, jnp.float32),
        ],
        in_specs=[pl.BlockSpec(memory_space=pltpu.SMEM)]
        + [pl.BlockSpec(memory_space=pltpu.VMEM)] * 6,
        out_specs=[
            pl.BlockSpec(memory_space=pltpu.VMEM),
            pl.BlockSpec(memory_space=pltpu.SMEM),
            pl.BlockSpec(memory_space=pltpu.VMEM),
        ],
        scratch_shapes=[pltpu.VMEM((8, 33, 8, 128), jnp.float32)],
        compiler_params=pltpu.CompilerParams(vmem_limit_bytes=32 << 20),
        cost_estimate=cost(1),
    )(info, *pieces, *rows)


def score_last(info, units, slots, shifts, rows, sums):
    return pl.pallas_call(
        functools.partial(last_kernel, shifts),
        out_shape=jax.ShapeDtypeStruct((8, 8, 128), jnp.float32),
        in_specs=[pl.BlockSpec(memory_space=pltpu.SMEM)] * 2
        + [pl.BlockSpec(memory_space=pltpu.VMEM)] * (2 + len(rows)),
        out_specs=pl.BlockSpec(memory_space=pltpu.VMEM),
        scratch_shapes=[pltpu.VMEM(SUMS, jnp.float32), pltpu.VMEM((8, 33, 8, 128), jnp.float32)],
        compiler_params=pltpu.CompilerParams(vmem_limit_bytes=32 << 20),
        cost_estimate=cost(len(shifts)),
    )(info, units, slots, *rows, sums)


def place_kernel(r_ref, o_ref):
    for g in range(4):
        o_ref[8 * g : 8 * g + 8, :] = jnp.concatenate(
            [r_ref[s][:, 32 * g : 32 * g + 32] for s in range(8)], axis=1
        )


def place(received):
    return pl.pallas_call(
        place_kernel,
        out_shape=jax.ShapeDtypeStruct((32, 256), jnp.float32),
        in_specs=[pl.BlockSpec(memory_space=pltpu.VMEM)],
        out_specs=pl.BlockSpec(memory_space=pltpu.VMEM),
    )(received)


def per_device(queries, passages, lengths):
    own = queries.reshape(256, 128)
    info = jnp.stack([lax.axis_index(name) for name in ("z", "yhi", "core", "x", "ylo")]).astype(jnp.int32)

    near = [own] + [lax.ppermute(own, PLANE, along(True, k)) for k in SHIFTS[1:]]
    filled = with_lengths(passages, lengths)
    once = on_x(filled, 1)
    moved = [filled, once, on_x(filled, -1), on_x(once, 1)]
    block = jnp.stack(near)
    mine = [lax.ppermute(block, PLANE, along(False, k)) for k in SHIFTS[1:]]
    slots, units, sums = score_first(info, moved, (block, to_core(block)))
    sums, mine[2] = lax.optimization_barrier((sums, mine[2]))
    rows = [w for v in mine for w in (v, to_core(v))]
    terms = score_last(info, units, slots, (1, 2, 3), rows, sums)
    received = lax.all_to_all(terms, ("z", "yhi"), 0, 0, tiled=True)
    return place(received)


def solution(mesh):
    fine = Mesh(mesh.devices.reshape(SIZES), NAMES)
    corpus = ("z", "yhi", "x")
    query = ("ylo", "core")
    return jax.shard_map(
        per_device,
        mesh=fine,
        in_specs=(P(corpus, query, None), P(query + corpus, None, None), P(query + corpus)),
        out_specs=P(corpus, query),
        check_vma=False,
    )
```

```python
import functools

import jax
import jax.numpy as jnp
from jax import lax
from jax.experimental import pallas as pl
from jax.experimental.pallas import tpu as pltpu
from jax.sharding import Mesh
from jax.sharding import PartitionSpec as P

NAMES = ("ylo", "core", "z", "yhi", "x")
SIZES = (2, 2, 4, 2, 4)
PLANE = ("ylo", "core", "z", "yhi")
OWN, SLOTS, WIDTH = 8, 128, 128
DEPTH = 16
LOWEST = -3.0e38


def plane_pairs(move):
    def index(ylo, core, z, yhi):
        return ((ylo * 2 + core) * 4 + z) * 2 + yhi

    pairs = []
    for ylo in range(2):
        for core in range(2):
            for z in range(4):
                for yhi in range(2):
                    y2, core2, z2 = move(2 * yhi + ylo, core, z)
                    pairs.append((index(ylo, core, z, yhi), index(y2 % 2, core2, z2, y2 // 2)))
    return pairs


def along(first, mask):
    def move(y, core, z):
        if (core == 0) == first:
            return y ^ mask, core, z
        return y, core, z ^ mask

    return plane_pairs(move)


def to_core(v):
    return lax.ppermute(v, "core", [(0, 1), (1, 0)])


def on_x(v, mask, other_mask):
    pairs = [
        (core * 4 + i, core * 4 + (i ^ (mask if core == 0 else other_mask)))
        for core in range(2)
        for i in range(4)
    ]
    return lax.ppermute(v, ("core", "x"), pairs)


def with_lengths(passages, lengths):
    tail = jnp.pad(lengths.astype(passages.dtype), (0, WIDTH - OWN))
    return jnp.concatenate(
        [passages.reshape(OWN * SLOTS, WIDTH), jnp.broadcast_to(tail, (16, WIDTH))], axis=0
    )


def best_dots(w_ref, p_ref, m_ref, s_ref, unit_ref, turns, *acc):
    acc = (acc[:DEPTH], acc[DEPTH:])
    nothing = jnp.zeros((16, 128), jnp.bfloat16)

    def push(g):
        for u in range(2):
            pltpu.matmul_push_rhs(w_ref[g * 2 + u], 0, u, transpose=True)

    def issue(unit, j, fresh=False):
        slots = p_ref[pl.ds(pl.multiple_of(unit, 16), 16), :]
        lhs = jnp.concatenate(
            [
                jnp.concatenate([slots, nothing], axis=1),
                jnp.concatenate([nothing, slots], axis=1),
            ],
            axis=0,
        )
        for u in range(2):
            pltpu.matmul_acc_lhs(acc[u][j], lhs, load_staged_rhs=0 if fresh else None)

    def take(unit, j):
        at = lax.shift_right_logical(unit, 7)
        begin = jnp.where(lax.bitwise_and(unit, 127) == 0, 32, at)
        tops = []
        held = [m_ref[b, begin] for b in range(8)]
        for u in range(2):
            d = pltpu.matmul_pop(acc[u][j])
            for half in range(2):
                top = jnp.maximum(d[16 * half : 16 * half + 8], d[16 * half + 8 : 16 * half + 16])
                tops += [top[:, 0:128], top[:, 128:256]]
        for b in range(8):
            m_ref[b, at] = jnp.maximum(held[b], tops[b])

    m_ref[:, 32] = jnp.full((8, 8, 128), LOWEST, jnp.float32)
    push(0)
    for j in range(DEPTH):
        issue(unit_ref[j], j, fresh=j == 0)

    def group(g, carry):

        def turn(t, c):
            for j in range(DEPTH):
                take(unit_ref[t * DEPTH + j], j)
                issue(unit_ref[t * DEPTH + DEPTH + j], j)
            return c

        lax.fori_loop(0, turns - 1, turn, 0)
        push(jnp.minimum(g + 1, 7))
        last = (turns - 1) * DEPTH
        for j in range(DEPTH):
            take(unit_ref[last + j], j)
            issue(unit_ref[j], j, fresh=j == 0)
        rows_ref = m_ref.reshape(8, 264, 128)
        for o in range(4):
            for side in range(2):
                total = None
                for b in range(side, 8, 2):
                    top = rows_ref[b, pl.ds(64 * o, 8, stride=8), :]
                    for i in range(1, 8):
                        top = jnp.maximum(top, rows_ref[b, pl.ds(64 * o + i, 8, stride=8), :])
                    total = top if total is None else total + top
                s_ref[g, 8 * o : 8 * o + 8, 128 * side : 128 * side + 128] = total
        return carry

    lax.fori_loop(0, 8, group, 0)
    for u in range(2):
        for j in range(DEPTH):
            m_ref[0, 0] = pltpu.matmul_pop(acc[u][j])[0:8, 0:128]


def score_kernel(info_ref, *refs):
    rows, pieces, out_ref = refs[:8], refs[8:12], refs[12]
    w_ref, p_ref, m_ref, s_ref, unit_ref = refs[13:]
    z, yhi, core, x = (info_ref[i] for i in range(4))

    for kind in range(2):

        @pl.when(core == kind)
        def _():
            for a in range(8):
                for j in range(4):
                    same = (a < 4) == (kind == 0)
                    dz, dy = (a % 4, j) if same else (j, a % 4)
                    h = dy // 2
                    half = 128 * (dy % 2)
                    w_ref[(dz * 2 + h) * 2 + a // 4, :, half : half + 128] = rows[a][j]

    count = jnp.int32(0)
    for m in range(4):
        from_x = lax.bitwise_xor(x, jnp.where(core == 0, (0, 1, 3, 2)[m], (0, 3, 1, 2)[m]))
        p_ref[pl.ds(pl.multiple_of(from_x * 1024, 1024), 1024), :] = pieces[m][0:1024, :]
        lengths = pieces[m][1024:1040, :].astype(jnp.float32)[0:8].astype(jnp.int32)
        units = lax.shift_right_logical(lengths + 15, 4)
        for i in range(OWN):
            for n in range(8):
                unit_ref[count + n] = from_x * 1024 + i * SLOTS + n * 16
            count = count + units[0, i]
            used = units[0, i]
            last = pl.multiple_of(from_x * 1024 + i * SLOTS + (used - 1) * 16, 16)
            both = p_ref[pl.ds(last, 16), :].astype(jnp.float32)
            second = jnp.where(lengths[0, i] == used * 16, both[8:16], both[0:8])
            p_ref[pl.ds(last, 16), :] = jnp.concatenate([both[0:8], second], axis=0).astype(p_ref.dtype)
    for i in range(DEPTH):
        unit_ref[count + i] = unit_ref[count - 1]
    turns = lax.div(count + DEPTH - 1, DEPTH)

    pl.run_scoped(
        functools.partial(best_dots, w_ref, p_ref, m_ref, s_ref, unit_ref, turns),
        *[pltpu.ACC(u)((32, 256), jnp.float32) for u in range(2) for _ in range(DEPTH)],
    )

    lane = lax.broadcasted_iota(jnp.int32, (32, 256), 1)
    row = lax.broadcasted_iota(jnp.int32, (32, 256), 0)
    pick = jnp.where(lane // 8 == row, 1.0 / 32, 0.0).astype(jnp.bfloat16)
    rest = s_ref[...].reshape(256, 256)
    parts = []
    for _ in range(3):
        parts.append(rest.astype(jnp.bfloat16))
        rest = rest - parts[-1].astype(jnp.float32)

    def add_up(acc):
        for part in parts:
            pltpu.matmul_push_rhs(part, 0, 0, transpose=True)
            pltpu.matmul_acc_lhs(acc, pick, load_staged_rhs=0)
        return pltpu.matmul_pop(acc)

    r = pl.run_scoped(add_up, pltpu.ACC(0)((32, 256), jnp.float32))
    for g in range(8):
        c = r[:, 32 * g : 32 * g + 32]
        place = lax.bitwise_xor(z * 2 + yhi, g)
        out_ref[place] = jnp.concatenate([c[0:8], c[8:16], c[16:24], c[24:32]], axis=1)


def score(info, rows, pieces):
    return pl.pallas_call(
        score_kernel,
        out_shape=jax.ShapeDtypeStruct((8, 8, 128), jnp.float32),
        in_specs=[pl.BlockSpec(memory_space=pltpu.SMEM)]
        + [pl.BlockSpec(memory_space=pltpu.VMEM)] * 12,
        out_specs=pl.BlockSpec(memory_space=pltpu.VMEM),
        scratch_shapes=[
            pltpu.VMEM((16, 256, 256), jnp.bfloat16),
            pltpu.VMEM((4096, 128), jnp.bfloat16),
            pltpu.VMEM((8, 33, 8, 128), jnp.float32),
            pltpu.VMEM((8, 32, 256), jnp.float32),
            pltpu.SMEM((256 + DEPTH,), jnp.int32),
        ],
        compiler_params=pltpu.CompilerParams(vmem_limit_bytes=32 << 20),
    )(info, *rows, *pieces)


def place_kernel(r_ref, o_ref):
    for g in range(4):
        o_ref[8 * g : 8 * g + 8, :] = jnp.concatenate(
            [r_ref[s][:, 32 * g : 32 * g + 32] for s in range(8)], axis=1
        )


def place(received):
    return pl.pallas_call(
        place_kernel,
        out_shape=jax.ShapeDtypeStruct((32, 256), jnp.float32),
        in_specs=[pl.BlockSpec(memory_space=pltpu.VMEM)],
        out_specs=pl.BlockSpec(memory_space=pltpu.VMEM),
    )(received)


def per_device(queries, passages, lengths):
    own = queries.reshape(256, 128)
    info = jnp.stack([lax.axis_index(name) for name in ("z", "yhi", "core", "x")]).astype(jnp.int32)

    near = [own] + [lax.ppermute(own, PLANE, along(True, k)) for k in range(1, 4)]
    filled = with_lengths(passages, lengths)
    once = on_x(filled, 1, 3)
    moved = [filled, once, on_x(filled, 3, 1), on_x(once, 3, 1)]
    block = jnp.stack(near)
    mine = [block] + [lax.ppermute(block, PLANE, along(False, k)) for k in range(1, 4)]
    other = [to_core(v) for v in mine]
    terms = score(info, mine + other, moved)
    received = lax.all_to_all(terms, ("z", "yhi"), 0, 0, tiled=True)
    return place(received)


def solution(mesh):
    fine = Mesh(mesh.devices.reshape(SIZES), NAMES)
    corpus = ("z", "yhi", "x")
    query = ("ylo", "core")
    return jax.shard_map(
        per_device,
        mesh=fine,
        in_specs=(P(corpus, query, None), P(query + corpus, None, None), P(query + corpus)),
        out_specs=P(corpus, query),
        check_vma=False,
    )
```

```python
import functools

import jax
import jax.numpy as jnp
from jax import lax
from jax.experimental import pallas as pl
from jax.experimental.pallas import tpu as pltpu
from jax.sharding import Mesh
from jax.sharding import PartitionSpec as P

NAMES = ("ylo", "core", "z", "yhi", "x")
SIZES = (2, 2, 4, 2, 4)
PLANE = ("ylo", "core", "z", "yhi")
OWN, SLOTS, WIDTH = 8, 128, 128
PERMUTED = 4
DEPTH = 16
LOWEST = -3.0e38


def plane_pairs(move):
    def index(ylo, core, z, yhi):
        return ((ylo * 2 + core) * 4 + z) * 2 + yhi

    pairs = []
    for ylo in range(2):
        for core in range(2):
            for z in range(4):
                for yhi in range(2):
                    y2, core2, z2 = move(2 * yhi + ylo, core, z)
                    pairs.append((index(ylo, core, z, yhi), index(y2 % 2, core2, z2, y2 // 2)))
    return pairs


def along(first, mask):
    def move(y, core, z):
        if (core == 0) == first:
            return y ^ mask, core, z
        return y, core, z ^ mask

    return plane_pairs(move)


def to_core(v):
    return lax.ppermute(v, "core", [(0, 1), (1, 0)])


def on_x(v, mask, other_mask):
    pairs = [
        (core * 4 + i, core * 4 + (i ^ (mask if core == 0 else other_mask)))
        for core in range(2)
        for i in range(4)
    ]
    return lax.ppermute(v, ("core", "x"), pairs)


def with_lengths(passages, lengths):
    tail = jnp.pad(lengths.astype(passages.dtype), (0, WIDTH - OWN))
    return jnp.concatenate(
        [passages.reshape(-1, WIDTH), jnp.broadcast_to(tail, (16, WIDTH))], axis=0
    )


def best_dots(w_ref, p_ref, m_ref, s_ref, unit_ref, turns, *acc):
    acc = (acc[:DEPTH], acc[DEPTH:])
    nothing = jnp.zeros((16, 128), jnp.bfloat16)

    def push(g):
        for u in range(2):
            pltpu.matmul_push_rhs(w_ref[g * 2 + u], 0, u, transpose=True)

    def issue(unit, j, fresh=False):
        slots = p_ref[pl.ds(pl.multiple_of(unit, 16), 16), :]
        lhs = jnp.concatenate(
            [
                jnp.concatenate([slots, nothing], axis=1),
                jnp.concatenate([nothing, slots], axis=1),
            ],
            axis=0,
        )
        for u in range(2):
            pltpu.matmul_acc_lhs(acc[u][j], lhs, load_staged_rhs=0 if fresh else None)

    def take(unit, j):
        at = lax.shift_right_logical(unit, 7)
        begin = jnp.where(lax.bitwise_and(unit, 127) == 0, 32, at)
        tops = []
        held = [m_ref[b, begin] for b in range(8)]
        for u in range(2):
            d = pltpu.matmul_pop(acc[u][j])
            for half in range(2):
                top = jnp.maximum(d[16 * half : 16 * half + 8], d[16 * half + 8 : 16 * half + 16])
                tops += [top[:, 0:128], top[:, 128:256]]
        for b in range(8):
            m_ref[b, at] = jnp.maximum(held[b], tops[b])

    m_ref[:, 32] = jnp.full((8, 8, 128), LOWEST, jnp.float32)
    push(0)
    for j in range(DEPTH):
        issue(unit_ref[j], j, fresh=j == 0)

    def group(g, carry):

        def turn(t, c):
            for j in range(DEPTH):
                take(unit_ref[t * DEPTH + j], j)
                issue(unit_ref[t * DEPTH + DEPTH + j], j)
            return c

        lax.fori_loop(0, turns - 1, turn, 0)
        push(jnp.minimum(g + 1, 7))
        last = (turns - 1) * DEPTH
        for j in range(DEPTH):
            take(unit_ref[last + j], j)
            issue(unit_ref[j], j, fresh=j == 0)
        rows_ref = m_ref.reshape(8, 264, 128)
        for o in range(4):
            for side in range(2):
                total = None
                for b in range(side, 8, 2):
                    top = rows_ref[b, pl.ds(64 * o, 8, stride=8), :]
                    for i in range(1, 8):
                        top = jnp.maximum(top, rows_ref[b, pl.ds(64 * o + i, 8, stride=8), :])
                    total = top if total is None else total + top
                s_ref[g, 8 * o : 8 * o + 8, 128 * side : 128 * side + 128] = total
        return carry

    lax.fori_loop(0, 8, group, 0)
    for u in range(2):
        for j in range(DEPTH):
            m_ref[0, 0] = pltpu.matmul_pop(acc[u][j])[0:8, 0:128]


def score_kernel(info_ref, *refs):
    rows, pieces, rest_ref, out_ref = refs[:8], refs[8:12], refs[12], refs[13]
    w_ref, p_ref, m_ref, s_ref, unit_ref = refs[14:]
    z, yhi, core, x = (info_ref[i] for i in range(4))

    for kind in range(2):

        @pl.when(core == kind)
        def _():
            for a in range(8):
                for j in range(4):
                    same = (a < 4) == (kind == 0)
                    dz, dy = (a % 4, j) if same else (j, a % 4)
                    h = dy // 2
                    half = 128 * (dy % 2)
                    w_ref[(dz * 2 + h) * 2 + a // 4, :, half : half + 128] = rows[a][j]

    count = jnp.int32(0)
    cut = PERMUTED * SLOTS
    for i in range(4):
        p_ref[1024 * i + cut : 1024 * i + 1024, :] = rest_ref[i * (1024 - cut) : (i + 1) * (1024 - cut), :]
    for m in range(4):
        from_x = lax.bitwise_xor(x, jnp.where(core == 0, (0, 1, 3, 2)[m], (0, 3, 1, 2)[m]))
        p_ref[pl.ds(pl.multiple_of(from_x * 1024, 1024), cut), :] = pieces[m][0:cut, :]
        lengths = pieces[m][cut : cut + 16, :].astype(jnp.float32)[0:8].astype(jnp.int32)
        units = lax.shift_right_logical(lengths + 15, 4)
        for i in range(OWN):
            for n in range(8):
                unit_ref[count + n] = from_x * 1024 + i * SLOTS + n * 16
            count = count + units[0, i]
            used = units[0, i]
            last = pl.multiple_of(from_x * 1024 + i * SLOTS + (used - 1) * 16, 16)
            both = p_ref[pl.ds(last, 16), :].astype(jnp.float32)
            second = jnp.where(lengths[0, i] == used * 16, both[8:16], both[0:8])
            p_ref[pl.ds(last, 16), :] = jnp.concatenate([both[0:8], second], axis=0).astype(p_ref.dtype)
    for i in range(DEPTH):
        unit_ref[count + i] = unit_ref[count - 1]
    turns = lax.div(count + DEPTH - 1, DEPTH)

    pl.run_scoped(
        functools.partial(best_dots, w_ref, p_ref, m_ref, s_ref, unit_ref, turns),
        *[pltpu.ACC(u)((32, 256), jnp.float32) for u in range(2) for _ in range(DEPTH)],
    )

    lane = lax.broadcasted_iota(jnp.int32, (32, 256), 1)
    row = lax.broadcasted_iota(jnp.int32, (32, 256), 0)
    pick = jnp.where(lane // 8 == row, 1.0 / 32, 0.0).astype(jnp.bfloat16)
    rest = s_ref[...].reshape(256, 256)
    parts = []
    for _ in range(3):
        parts.append(rest.astype(jnp.bfloat16))
        rest = rest - parts[-1].astype(jnp.float32)

    def add_up(acc):
        for part in parts:
            pltpu.matmul_push_rhs(part, 0, 0, transpose=True)
            pltpu.matmul_acc_lhs(acc, pick, load_staged_rhs=0)
        return pltpu.matmul_pop(acc)

    r = pl.run_scoped(add_up, pltpu.ACC(0)((32, 256), jnp.float32))
    for g in range(8):
        c = r[:, 32 * g : 32 * g + 32]
        place = lax.bitwise_xor(z * 2 + yhi, g)
        out_ref[place] = jnp.concatenate([c[0:8], c[8:16], c[16:24], c[24:32]], axis=1)


def score(info, rows, pieces, rest):
    return pl.pallas_call(
        score_kernel,
        out_shape=jax.ShapeDtypeStruct((8, 8, 128), jnp.float32),
        in_specs=[pl.BlockSpec(memory_space=pltpu.SMEM)]
        + [pl.BlockSpec(memory_space=pltpu.VMEM)] * 13,
        out_specs=pl.BlockSpec(memory_space=pltpu.VMEM),
        scratch_shapes=[
            pltpu.VMEM((16, 256, 256), jnp.bfloat16),
            pltpu.VMEM((4096, 128), jnp.bfloat16),
            pltpu.VMEM((8, 33, 8, 128), jnp.float32),
            pltpu.VMEM((8, 32, 256), jnp.float32),
            pltpu.SMEM((256 + DEPTH,), jnp.int32),
        ],
        compiler_params=pltpu.CompilerParams(vmem_limit_bytes=32 << 20),
    )(info, *rows, *pieces, rest)


def place_kernel(r_ref, o_ref):
    for g in range(4):
        o_ref[8 * g : 8 * g + 8, :] = jnp.concatenate(
            [r_ref[s][:, 32 * g : 32 * g + 32] for s in range(8)], axis=1
        )


def place(received):
    return pl.pallas_call(
        place_kernel,
        out_shape=jax.ShapeDtypeStruct((32, 256), jnp.float32),
        in_specs=[pl.BlockSpec(memory_space=pltpu.VMEM)],
        out_specs=pl.BlockSpec(memory_space=pltpu.VMEM),
    )(received)


def per_device(queries, passages, lengths):
    own = queries.reshape(256, 128)
    info = jnp.stack([lax.axis_index(name) for name in ("z", "yhi", "core", "x")]).astype(jnp.int32)

    near = [own] + [lax.ppermute(own, PLANE, along(True, k)) for k in range(1, 4)]
    filled = with_lengths(passages[:PERMUTED], lengths)
    rest = lax.all_gather(passages[PERMUTED:].reshape(-1, WIDTH), "x", axis=0, tiled=True)
    once = on_x(filled, 1, 3)
    moved = [filled, once, on_x(filled, 3, 1), on_x(once, 3, 1)]
    block = jnp.stack(near)
    mine = [block] + [lax.ppermute(block, PLANE, along(False, k)) for k in range(1, 4)]
    other = [to_core(v) for v in mine]
    terms = score(info, mine + other, moved, rest)
    received = lax.all_to_all(terms, ("z", "yhi"), 0, 0, tiled=True)
    return place(received)


def solution(mesh):
    fine = Mesh(mesh.devices.reshape(SIZES), NAMES)
    corpus = ("z", "yhi", "x")
    query = ("ylo", "core")
    return jax.shard_map(
        per_device,
        mesh=fine,
        in_specs=(P(corpus, query, None), P(query + corpus, None, None), P(query + corpus)),
        out_specs=P(corpus, query),
        check_vma=False,
    )
```

```python
import functools

import jax
import jax.numpy as jnp
from jax import lax
from jax.experimental import pallas as pl
from jax.experimental.pallas import tpu as pltpu
from jax.sharding import Mesh
from jax.sharding import PartitionSpec as P

NAMES = ("ylo", "core", "z", "yhi", "x")
SIZES = (2, 2, 4, 2, 4)
PLANE = ("ylo", "core", "z", "yhi")
OWN, SLOTS, WIDTH = 8, 128, 128
DEPTH = 16
LOWEST = -3.0e38


def plane_pairs(move):
    def index(ylo, core, z, yhi):
        return ((ylo * 2 + core) * 4 + z) * 2 + yhi

    pairs = []
    for ylo in range(2):
        for core in range(2):
            for z in range(4):
                for yhi in range(2):
                    y2, core2, z2 = move(2 * yhi + ylo, core, z)
                    pairs.append((index(ylo, core, z, yhi), index(y2 % 2, core2, z2, y2 // 2)))
    return pairs


def along(first, mask):
    def move(y, core, z):
        if (core == 0) == first:
            return y ^ mask, core, z
        return y, core, z ^ mask

    return plane_pairs(move)


def to_core(v):
    return lax.ppermute(v, "core", [(0, 1), (1, 0)])


def on_x(v, mask, other_mask):
    pairs = [
        (core * 4 + i, core * 4 + (i ^ (mask if core == 0 else other_mask)))
        for core in range(2)
        for i in range(4)
    ]
    return lax.ppermute(v, ("core", "x"), pairs)


def with_lengths(passages, lengths):
    tail = jnp.pad(lengths.astype(passages.dtype), (0, WIDTH - OWN))
    slot = lax.broadcasted_iota(jnp.int32, passages.shape, 1)
    before = jnp.concatenate([passages[:, :8], passages[:, :-8]], axis=1)
    filled = jnp.where(slot < lengths[:, None, None], passages, before)
    return jnp.concatenate(
        [filled.reshape(OWN * SLOTS, WIDTH), jnp.broadcast_to(tail, (16, WIDTH))], axis=0
    )


def best_dots(rows, places, p_ref, m_ref, s_ref, unit_ref, turns, *acc):
    acc = (acc[:DEPTH], acc[DEPTH:])
    nothing = jnp.zeros((16, 128), jnp.bfloat16)

    def push(g):
        for u in range(2):
            held = jnp.concatenate([ref[j] for ref, j in rows[g][2 * u : 2 * u + 2]], axis=1)
            pltpu.matmul_push_rhs(held, 0, u, transpose=True)

    def issue(unit, j, fresh=False):
        slots = p_ref[pl.ds(pl.multiple_of(unit, 16), 16), :]
        lhs = jnp.concatenate(
            [
                jnp.concatenate([slots, nothing], axis=1),
                jnp.concatenate([nothing, slots], axis=1),
            ],
            axis=0,
        )
        for u in range(2):
            pltpu.matmul_acc_lhs(acc[u][j], lhs, load_staged_rhs=0 if fresh else None)

    def take(unit, j):
        at = lax.shift_right_logical(unit, 7)
        begin = jnp.where(lax.bitwise_and(unit, 127) == 0, 32, at)
        tops = []
        held = [m_ref[b, begin] for b in range(8)]
        for u in range(2):
            d = pltpu.matmul_pop(acc[u][j])
            for half in range(2):
                top = jnp.maximum(d[16 * half : 16 * half + 8], d[16 * half + 8 : 16 * half + 16])
                tops += [top[:, 0:128], top[:, 128:256]]
        for b in range(8):
            m_ref[b, at] = jnp.maximum(held[b], tops[b])

    def turn(t, c):
        for j in range(DEPTH):
            take(unit_ref[t * DEPTH + j], j)
            issue(unit_ref[t * DEPTH + DEPTH + j], j)
        return c

    m_ref[:, 32] = jnp.full((8, 8, 128), LOWEST, jnp.float32)
    rows_ref = m_ref.reshape(8, 264, 128)
    push(0)
    for j in range(DEPTH):
        issue(unit_ref[j], j, fresh=j == 0)
    for g in range(len(rows)):
        lax.fori_loop(0, turns - 1, turn, 0)
        more = g + 1 < len(rows)
        if more:
            push(g + 1)
        last = (turns - 1) * DEPTH
        for j in range(DEPTH):
            take(unit_ref[last + j], j)
            if more:
                issue(unit_ref[j], j, fresh=j == 0)
        for o in range(4):
            for b in range(8):
                top = rows_ref[b, pl.ds(64 * o, 8, stride=8), :]
                for i in range(1, 8):
                    top = jnp.maximum(top, rows_ref[b, pl.ds(64 * o + i, 8, stride=8), :])
                lanes = slice(128 * (b % 2), 128 * (b % 2) + 128)
                s_ref[places[g][b // 2], 8 * o : 8 * o + 8, lanes] += top


def score_kernel(info_ref, *refs):
    rows, pieces, out_ref = refs[:8], refs[8:12], refs[12]
    p_ref, m_ref, s_ref, unit_ref = refs[13:]
    z, yhi, core, x = (info_ref[i] for i in range(4))

    groups, places = [], []
    for k in range(4):
        for j in (0, 2):
            groups.append([(rows[c + k], e) for c in (0, 4) for e in (j, j + 1)])
            by_chain = [[k * 2 + e // 2, e * 2 + k // 2] for e in (j, j + 1)]
            places.append(
                [jnp.where(chain == 0, p, q) for chain in (core, 1 - core) for p, q in by_chain]
            )

    count = jnp.int32(0)
    for m in range(4):
        from_x = lax.bitwise_xor(x, jnp.where(core == 0, (0, 1, 3, 2)[m], (0, 3, 1, 2)[m]))
        p_ref[pl.ds(pl.multiple_of(from_x * 1024, 1024), 1024), :] = pieces[m][0:1024, :]
        lengths = pieces[m][1024:1040, :].astype(jnp.float32)[0:8].astype(jnp.int32)
        units = lax.shift_right_logical(lengths + 15, 4)
        for i in range(OWN):
            for n in range(8):
                unit_ref[count + n] = from_x * 1024 + i * SLOTS + n * 16
            count = count + units[0, i]
    for i in range(DEPTH):
        unit_ref[count + i] = unit_ref[count - 1]
    turns = lax.div(count + DEPTH - 1, DEPTH)

    s_ref[...] = jnp.zeros_like(s_ref)
    pl.run_scoped(
        functools.partial(best_dots, groups, places, p_ref, m_ref, s_ref, unit_ref, turns),
        *[pltpu.ACC(u)((32, 256), jnp.float32) for u in range(2) for _ in range(DEPTH)],
    )

    lane = lax.broadcasted_iota(jnp.int32, (32, 256), 1)
    row = lax.broadcasted_iota(jnp.int32, (32, 256), 0)
    pick = jnp.where(lane // 8 == row, 1.0 / 32, 0.0).astype(jnp.bfloat16)
    rest = s_ref[...].reshape(256, 256)
    parts = []
    for _ in range(3):
        parts.append(rest.astype(jnp.bfloat16))
        rest = rest - parts[-1].astype(jnp.float32)

    def add_up(acc):
        for part in parts:
            pltpu.matmul_push_rhs(part, 0, 0, transpose=True)
            pltpu.matmul_acc_lhs(acc, pick, load_staged_rhs=0)
        return pltpu.matmul_pop(acc)

    r = pl.run_scoped(add_up, pltpu.ACC(0)((32, 256), jnp.float32))
    for g in range(8):
        c = r[:, 32 * g : 32 * g + 32]
        place = lax.bitwise_xor(z * 2 + yhi, g)
        out_ref[place] = jnp.concatenate([c[0:8], c[8:16], c[16:24], c[24:32]], axis=1)


def score(info, rows, pieces):
    return pl.pallas_call(
        score_kernel,
        out_shape=jax.ShapeDtypeStruct((8, 8, 128), jnp.float32),
        in_specs=[pl.BlockSpec(memory_space=pltpu.SMEM)]
        + [pl.BlockSpec(memory_space=pltpu.VMEM)] * 12,
        out_specs=pl.BlockSpec(memory_space=pltpu.VMEM),
        scratch_shapes=[
            pltpu.VMEM((4096, 128), jnp.bfloat16),
            pltpu.VMEM((8, 33, 8, 128), jnp.float32),
            pltpu.VMEM((8, 32, 256), jnp.float32),
            pltpu.SMEM((256 + DEPTH,), jnp.int32),
        ],
        compiler_params=pltpu.CompilerParams(vmem_limit_bytes=32 << 20),
    )(info, *rows, *pieces)


def place_kernel(r_ref, o_ref):
    for g in range(4):
        o_ref[8 * g : 8 * g + 8, :] = jnp.concatenate(
            [r_ref[s][:, 32 * g : 32 * g + 32] for s in range(8)], axis=1
        )


def place(received):
    return pl.pallas_call(
        place_kernel,
        out_shape=jax.ShapeDtypeStruct((32, 256), jnp.float32),
        in_specs=[pl.BlockSpec(memory_space=pltpu.VMEM)],
        out_specs=pl.BlockSpec(memory_space=pltpu.VMEM),
    )(received)


def per_device(queries, passages, lengths):
    own = queries.reshape(256, 128)
    info = jnp.stack([lax.axis_index(name) for name in ("z", "yhi", "core", "x")]).astype(jnp.int32)

    near = [own] + [lax.ppermute(own, PLANE, along(True, k)) for k in range(1, 4)]
    filled = with_lengths(passages, lengths)
    once = on_x(filled, 1, 3)
    moved = [filled, once, on_x(filled, 3, 1), on_x(once, 3, 1)]
    block = jnp.stack(near)
    mine = [block] + [lax.ppermute(block, PLANE, along(False, k)) for k in range(1, 4)]
    other = [to_core(v) for v in mine]
    terms = score(info, mine + other, moved)
    received = lax.all_to_all(terms, ("z", "yhi"), 0, 0, tiled=True)
    return place(received)


def solution(mesh):
    fine = Mesh(mesh.devices.reshape(SIZES), NAMES)
    corpus = ("z", "yhi", "x")
    query = ("ylo", "core")
    return jax.shard_map(
        per_device,
        mesh=fine,
        in_specs=(P(corpus, query, None), P(query + corpus, None, None), P(query + corpus)),
        out_specs=P(corpus, query),
        check_vma=False,
    )
```

```python
import functools

import jax
import jax.numpy as jnp
from jax import lax
from jax.experimental import pallas as pl
from jax.experimental.pallas import tpu as pltpu
from jax.sharding import Mesh
from jax.sharding import PartitionSpec as P

NAMES = ("ylo", "core", "z", "yhi", "x")
SIZES = (2, 2, 4, 2, 4)
PLANE = ("ylo", "core", "z", "yhi")
OWN, SLOTS, WIDTH = 8, 128, 128
DEPTH = 16
LOWEST = -3.0e38


def plane_pairs(move):
    def index(ylo, core, z, yhi):
        return ((ylo * 2 + core) * 4 + z) * 2 + yhi

    pairs = []
    for ylo in range(2):
        for core in range(2):
            for z in range(4):
                for yhi in range(2):
                    y2, core2, z2 = move(2 * yhi + ylo, core, z)
                    pairs.append((index(ylo, core, z, yhi), index(y2 % 2, core2, z2, y2 // 2)))
    return pairs


def along(first, mask):
    def move(y, core, z):
        if (core == 0) == first:
            return y ^ mask, core, z
        return y, core, z ^ mask

    return plane_pairs(move)


def to_core(v):
    return lax.ppermute(v, "core", [(0, 1), (1, 0)])


def on_x(v, mask, other_mask):
    pairs = [
        (core * 4 + i, core * 4 + (i ^ (mask if core == 0 else other_mask)))
        for core in range(2)
        for i in range(4)
    ]
    return lax.ppermute(v, ("core", "x"), pairs)


def with_lengths(passages, lengths):
    tail = jnp.pad(lengths.astype(passages.dtype), (0, WIDTH - OWN))
    slot = lax.broadcasted_iota(jnp.int32, passages.shape, 1)
    before = jnp.concatenate([passages[:, :8], passages[:, :-8]], axis=1)
    filled = jnp.where(slot < lengths[:, None, None], passages, before)
    return jnp.concatenate(
        [filled.reshape(OWN * SLOTS, WIDTH), jnp.broadcast_to(tail, (16, WIDTH))], axis=0
    )


def best_dots(rows, places, p_ref, m_ref, s_ref, unit_ref, turns, *acc):
    acc = (acc[:DEPTH], acc[DEPTH:])
    nothing = jnp.zeros((16, 128), jnp.bfloat16)

    def push(g):
        for u in range(2):
            held = jnp.concatenate([ref[j] for ref, j in rows[g][2 * u : 2 * u + 2]], axis=1)
            pltpu.matmul_push_rhs(held, 0, u, transpose=True)

    def issue(unit, j, fresh=False):
        slots = p_ref[pl.ds(pl.multiple_of(unit, 16), 16), :]
        lhs = jnp.concatenate(
            [
                jnp.concatenate([slots, nothing], axis=1),
                jnp.concatenate([nothing, slots], axis=1),
            ],
            axis=0,
        )
        for u in range(2):
            pltpu.matmul_acc_lhs(acc[u][j], lhs, load_staged_rhs=0 if fresh else None)

    def take(unit, j):
        at = lax.shift_right_logical(unit, 7)
        begin = jnp.where(lax.bitwise_and(unit, 127) == 0, 32, at)
        tops = []
        held = [m_ref[b, begin] for b in range(8)]
        for u in range(2):
            d = pltpu.matmul_pop(acc[u][j])
            for half in range(2):
                top = jnp.maximum(d[16 * half : 16 * half + 8], d[16 * half + 8 : 16 * half + 16])
                tops += [top[:, 0:128], top[:, 128:256]]
        for b in range(8):
            m_ref[b, at] = jnp.maximum(held[b], tops[b])

    def turn(t, c):
        for j in range(DEPTH):
            take(unit_ref[t * DEPTH + j], j)
            issue(unit_ref[t * DEPTH + DEPTH + j], j)
        return c

    m_ref[:, 32] = jnp.full((8, 8, 128), LOWEST, jnp.float32)
    rows_ref = m_ref.reshape(8, 264, 128)
    push(0)
    for j in range(DEPTH):
        issue(unit_ref[j], j, fresh=j == 0)
    for g in range(len(rows)):
        lax.fori_loop(0, turns - 1, turn, 0)
        more = g + 1 < len(rows)
        if more:
            push(g + 1)
        last = (turns - 1) * DEPTH
        for j in range(DEPTH):
            take(unit_ref[last + j], j)
            if more:
                issue(unit_ref[j], j, fresh=j == 0)
        for o in range(4):
            for b in range(8):
                top = rows_ref[b, pl.ds(64 * o, 8, stride=8), :]
                for i in range(1, 8):
                    top = jnp.maximum(top, rows_ref[b, pl.ds(64 * o + i, 8, stride=8), :])
                lanes = slice(128 * (b % 2), 128 * (b % 2) + 128)
                s_ref[places[g][b // 2], 8 * o : 8 * o + 8, lanes] += top


def score_kernel(info_ref, *refs):
    rows, pieces, outs = refs[:8], refs[8:12], refs[12:20]
    p_ref, m_ref, s_ref, unit_ref = refs[20:]
    core, x = info_ref[2], info_ref[3]

    groups, places = [], []
    for k in range(4):
        for j in (0, 2):
            groups.append([(rows[c + k], e) for c in (0, 4) for e in (j, j + 1)])
            by_chain = [[k * 2 + e // 2, e * 2 + k // 2] for e in (j, j + 1)]
            places.append(
                [jnp.where(chain == 0, p, q) for chain in (core, 1 - core) for p, q in by_chain]
            )

    count = jnp.int32(0)
    for m in range(4):
        from_x = lax.bitwise_xor(x, jnp.where(core == 0, (0, 1, 3, 2)[m], (0, 3, 1, 2)[m]))
        p_ref[pl.ds(pl.multiple_of(from_x * 1024, 1024), 1024), :] = pieces[m][0:1024, :]
        lengths = pieces[m][1024:1040, :].astype(jnp.float32)[0:8].astype(jnp.int32)
        units = lax.shift_right_logical(lengths + 15, 4)
        for i in range(OWN):
            for n in range(8):
                unit_ref[count + n] = from_x * 1024 + i * SLOTS + n * 16
            count = count + units[0, i]
    for i in range(DEPTH):
        unit_ref[count + i] = unit_ref[count - 1]
    turns = lax.div(count + DEPTH - 1, DEPTH)

    s_ref[...] = jnp.zeros_like(s_ref)
    pl.run_scoped(
        functools.partial(best_dots, groups, places, p_ref, m_ref, s_ref, unit_ref, turns),
        *[pltpu.ACC(u)((32, 256), jnp.float32) for u in range(2) for _ in range(DEPTH)],
    )

    lane = lax.broadcasted_iota(jnp.int32, (32, 256), 1)
    row = lax.broadcasted_iota(jnp.int32, (32, 256), 0)
    pick = jnp.where(lane // 8 == row, 1.0 / 32, 0.0).astype(jnp.bfloat16)
    rest = s_ref[...].reshape(256, 256)
    parts = []
    for _ in range(3):
        parts.append(rest.astype(jnp.bfloat16))
        rest = rest - parts[-1].astype(jnp.float32)

    def add_up(acc):
        for part in parts:
            pltpu.matmul_push_rhs(part, 0, 0, transpose=True)
            pltpu.matmul_acc_lhs(acc, pick, load_staged_rhs=0)
        return pltpu.matmul_pop(acc)

    r = pl.run_scoped(add_up, pltpu.ACC(0)((32, 256), jnp.float32))
    for g in range(8):
        c = r[:, 32 * g : 32 * g + 32]
        outs[g][...] = jnp.concatenate([c[0:8], c[8:16], c[16:24], c[24:32]], axis=1)


def score(info, rows, pieces):
    return pl.pallas_call(
        score_kernel,
        out_shape=[jax.ShapeDtypeStruct((8, 128), jnp.float32)] * 8,
        in_specs=[pl.BlockSpec(memory_space=pltpu.SMEM)]
        + [pl.BlockSpec(memory_space=pltpu.VMEM)] * 12,
        out_specs=[pl.BlockSpec(memory_space=pltpu.VMEM)] * 8,
        scratch_shapes=[
            pltpu.VMEM((4096, 128), jnp.bfloat16),
            pltpu.VMEM((8, 33, 8, 128), jnp.float32),
            pltpu.VMEM((8, 32, 256), jnp.float32),
            pltpu.SMEM((256 + DEPTH,), jnp.int32),
        ],
        compiler_params=pltpu.CompilerParams(vmem_limit_bytes=32 << 20),
    )(info, *rows, *pieces)


def place_kernel(info_ref, *refs):
    parts, o_ref, held_ref = refs[:8], refs[8], refs[9]
    for g in range(8):
        held_ref[lax.bitwise_xor(info_ref[0] * 2 + info_ref[1], g)] = parts[g][...]
    for g in range(4):
        o_ref[8 * g : 8 * g + 8, :] = jnp.concatenate(
            [held_ref[s][:, 32 * g : 32 * g + 32] for s in range(8)], axis=1
        )


def place(info, parts):
    return pl.pallas_call(
        place_kernel,
        out_shape=jax.ShapeDtypeStruct((32, 256), jnp.float32),
        in_specs=[pl.BlockSpec(memory_space=pltpu.SMEM)]
        + [pl.BlockSpec(memory_space=pltpu.VMEM)] * 8,
        out_specs=pl.BlockSpec(memory_space=pltpu.VMEM),
        scratch_shapes=[pltpu.VMEM((8, 8, 128), jnp.float32)],
    )(info, *parts)


def home(v, g):
    return lax.ppermute(v, ("z", "yhi"), [(i, i ^ g) for i in range(8)])


def per_device(queries, passages, lengths):
    own = queries.reshape(256, 128)
    info = jnp.stack([lax.axis_index(name) for name in ("z", "yhi", "core", "x")]).astype(jnp.int32)

    near = [own] + [lax.ppermute(own, PLANE, along(True, k)) for k in range(1, 4)]
    filled = with_lengths(passages, lengths)
    once = on_x(filled, 1, 3)
    moved = [filled, once, on_x(filled, 3, 1), on_x(once, 3, 1)]
    block = jnp.stack(near)
    mine = [block] + [lax.ppermute(block, PLANE, along(False, k)) for k in range(1, 4)]
    other = [to_core(v) for v in mine]
    terms = score(info, mine + other, moved)
    return place(info, [terms[0]] + [home(terms[g], g) for g in range(1, 8)])


def solution(mesh):
    fine = Mesh(mesh.devices.reshape(SIZES), NAMES)
    corpus = ("z", "yhi", "x")
    query = ("ylo", "core")
    return jax.shard_map(
        per_device,
        mesh=fine,
        in_specs=(P(corpus, query, None), P(query + corpus, None, None), P(query + corpus)),
        out_specs=P(corpus, query),
        check_vma=False,
    )
```

```python
import functools

import jax
import jax.numpy as jnp
from jax import lax
from jax.experimental import pallas as pl
from jax.experimental.pallas import tpu as pltpu
from jax.sharding import Mesh
from jax.sharding import PartitionSpec as P

NAMES = ("ylo", "core", "z", "yhi", "x")
SIZES = (2, 2, 4, 2, 4)
PLANE = ("ylo", "core", "z", "yhi")
OWN, SLOTS, WIDTH = 8, 128, 128
DEPTH = 16
LOWEST = -3.0e38


def plane_pairs(move):
    def index(ylo, core, z, yhi):
        return ((ylo * 2 + core) * 4 + z) * 2 + yhi

    pairs = []
    for ylo in range(2):
        for core in range(2):
            for z in range(4):
                for yhi in range(2):
                    y2, core2, z2 = move(2 * yhi + ylo, core, z)
                    pairs.append((index(ylo, core, z, yhi), index(y2 % 2, core2, z2, y2 // 2)))
    return pairs


def along(first, mask):
    def move(y, core, z):
        if (core == 0) == first:
            return y ^ mask, core, z
        return y, core, z ^ mask

    return plane_pairs(move)


def to_core(v):
    return lax.ppermute(v, "core", [(0, 1), (1, 0)])


def on_x(v, mask, other_mask):
    pairs = [
        (core * 4 + i, core * 4 + (i ^ (mask if core == 0 else other_mask)))
        for core in range(2)
        for i in range(4)
    ]
    return lax.ppermute(v, ("core", "x"), pairs)


def with_lengths(passages, lengths):
    tail = jnp.pad(lengths.astype(passages.dtype), (0, WIDTH - OWN))
    slot = lax.broadcasted_iota(jnp.int32, passages.shape, 1)
    before = jnp.concatenate([passages[:, :8], passages[:, :-8]], axis=1)
    filled = jnp.where(slot < lengths[:, None, None], passages, before)
    return jnp.concatenate(
        [filled.reshape(OWN * SLOTS, WIDTH), jnp.broadcast_to(tail, (16, WIDTH))], axis=0
    )


def best_dots(rows, places, p_ref, m_ref, s_ref, unit_ref, turns, *acc):
    acc = (acc[:DEPTH], acc[DEPTH:])
    nothing = jnp.zeros((16, 128), jnp.bfloat16)

    def push(g):
        for u in range(2):
            held = jnp.concatenate([ref[j] for ref, j in rows[g][2 * u : 2 * u + 2]], axis=1)
            pltpu.matmul_push_rhs(held, 0, u, transpose=True)

    def issue(unit, j, fresh=False):
        slots = p_ref[pl.ds(pl.multiple_of(unit, 16), 16), :]
        lhs = jnp.concatenate(
            [
                jnp.concatenate([slots, nothing], axis=1),
                jnp.concatenate([nothing, slots], axis=1),
            ],
            axis=0,
        )
        for u in range(2):
            pltpu.matmul_acc_lhs(acc[u][j], lhs, load_staged_rhs=0 if fresh else None)

    def take(unit, j):
        at = lax.shift_right_logical(unit, 7)
        begin = jnp.where(lax.bitwise_and(unit, 127) == 0, 32, at)
        tops = []
        held = [m_ref[b, begin] for b in range(8)]
        for u in range(2):
            d = pltpu.matmul_pop(acc[u][j])
            for half in range(2):
                top = jnp.maximum(d[16 * half : 16 * half + 8], d[16 * half + 8 : 16 * half + 16])
                tops += [top[:, 0:128], top[:, 128:256]]
        for b in range(8):
            m_ref[b, at] = jnp.maximum(held[b], tops[b])

    def turn(t, c):
        for j in range(DEPTH):
            take(unit_ref[t * DEPTH + j], j)
            issue(unit_ref[t * DEPTH + DEPTH + j], j)
        return c

    m_ref[:, 32] = jnp.full((8, 8, 128), LOWEST, jnp.float32)
    rows_ref = m_ref.reshape(8, 264, 128)
    push(0)
    for j in range(DEPTH):
        issue(unit_ref[j], j, fresh=j == 0)
    for g in range(len(rows)):
        lax.fori_loop(0, turns - 1, turn, 0)
        more = g + 1 < len(rows)
        if more:
            push(g + 1)
        last = (turns - 1) * DEPTH
        for j in range(DEPTH):
            take(unit_ref[last + j], j)
            if more:
                issue(unit_ref[j], j, fresh=j == 0)
        for o in range(4):
            for b in range(8):
                top = rows_ref[b, pl.ds(64 * o, 8, stride=8), :]
                for i in range(1, 8):
                    top = jnp.maximum(top, rows_ref[b, pl.ds(64 * o + i, 8, stride=8), :])
                lanes = slice(128 * (b % 2), 128 * (b % 2) + 128)
                s_ref[places[g][b // 2], 8 * o : 8 * o + 8, lanes] += top


def score_kernel(info_ref, *refs):
    rows, pieces, out_ref = refs[:8], refs[8:12], refs[12]
    p_ref, m_ref, s_ref, unit_ref = refs[13:]
    z, yhi, core, x = (info_ref[i] for i in range(4))

    groups, places = [], []
    for k in range(4):
        for j in (0, 2):
            groups.append([(rows[c + k], e) for c in (0, 4) for e in (j, j + 1)])
            by_chain = [[k * 2 + e // 2, e * 2 + k // 2] for e in (j, j + 1)]
            places.append(
                [jnp.where(chain == 0, p, q) for chain in (core, 1 - core) for p, q in by_chain]
            )

    count = jnp.int32(0)
    for m in range(4):
        from_x = lax.bitwise_xor(x, jnp.where(core == 0, (0, 1, 3, 2)[m], (0, 3, 1, 2)[m]))
        p_ref[pl.ds(pl.multiple_of(from_x * 1024, 1024), 1024), :] = pieces[m][0:1024, :]
        lengths = pieces[m][1024:1040, :].astype(jnp.float32)[0:8].astype(jnp.int32)
        units = lax.shift_right_logical(lengths + 15, 4)
        for i in range(OWN):
            for n in range(8):
                unit_ref[count + n] = from_x * 1024 + i * SLOTS + n * 16
            count = count + units[0, i]
    for i in range(DEPTH):
        unit_ref[count + i] = unit_ref[count - 1]
    turns = lax.div(count + DEPTH - 1, DEPTH)

    s_ref[...] = jnp.zeros_like(s_ref)
    pl.run_scoped(
        functools.partial(best_dots, groups, places, p_ref, m_ref, s_ref, unit_ref, turns),
        *[pltpu.ACC(u)((32, 256), jnp.float32) for u in range(2) for _ in range(DEPTH)],
    )

    lane = lax.broadcasted_iota(jnp.int32, (32, 256), 1)
    row = lax.broadcasted_iota(jnp.int32, (32, 256), 0)
    pick = jnp.where(lane // 8 == row, 1.0 / 32, 0.0).astype(jnp.bfloat16)
    rest = s_ref[...].reshape(256, 256)
    parts = []
    for _ in range(3):
        parts.append(rest.astype(jnp.bfloat16))
        rest = rest - parts[-1].astype(jnp.float32)

    def add_up(acc):
        for part in parts:
            pltpu.matmul_push_rhs(part, 0, 0, transpose=True)
            pltpu.matmul_acc_lhs(acc, pick, load_staged_rhs=0)
        return pltpu.matmul_pop(acc)

    r = pl.run_scoped(add_up, pltpu.ACC(0)((32, 256), jnp.float32))
    for g in range(8):
        c = r[:, 32 * g : 32 * g + 32]
        place = lax.bitwise_xor(z * 2 + yhi, g)
        out_ref[place] = jnp.concatenate([c[0:8], c[8:16], c[16:24], c[24:32]], axis=1)


def score(info, rows, pieces):
    return pl.pallas_call(
        score_kernel,
        out_shape=jax.ShapeDtypeStruct((8, 8, 128), jnp.float32),
        in_specs=[pl.BlockSpec(memory_space=pltpu.SMEM)]
        + [pl.BlockSpec(memory_space=pltpu.VMEM)] * 12,
        out_specs=pl.BlockSpec(memory_space=pltpu.VMEM),
        scratch_shapes=[
            pltpu.VMEM((4096, 128), jnp.bfloat16),
            pltpu.VMEM((8, 33, 8, 128), jnp.float32),
            pltpu.VMEM((8, 32, 256), jnp.float32),
            pltpu.SMEM((256 + DEPTH,), jnp.int32),
        ],
        compiler_params=pltpu.CompilerParams(vmem_limit_bytes=32 << 20),
    )(info, *rows, *pieces)


def place_kernel(r_ref, o_ref):
    for g in range(4):
        o_ref[8 * g : 8 * g + 8, :] = jnp.concatenate(
            [r_ref[s][:, 32 * g : 32 * g + 32] for s in range(8)], axis=1
        )


def place(received):
    return pl.pallas_call(
        place_kernel,
        out_shape=jax.ShapeDtypeStruct((32, 256), jnp.float32),
        in_specs=[pl.BlockSpec(memory_space=pltpu.VMEM)],
        out_specs=pl.BlockSpec(memory_space=pltpu.VMEM),
    )(received)


def per_device(queries, passages, lengths):
    own = queries.reshape(256, 128)
    info = jnp.stack([lax.axis_index(name) for name in ("z", "yhi", "core", "x")]).astype(jnp.int32)

    near = [own] + [lax.ppermute(own, PLANE, along(True, k)) for k in range(1, 4)]
    filled = with_lengths(passages, lengths)
    once = on_x(filled, 1, 3)
    once, later = lax.optimization_barrier((once, filled))
    moved = [filled, once, on_x(later, 3, 1), on_x(once, 3, 1)]
    block = jnp.stack(near)
    mine = [block] + [lax.ppermute(block, PLANE, along(False, k)) for k in range(1, 4)]
    other = [to_core(v) for v in mine]
    terms = score(info, mine + other, moved)
    received = lax.all_to_all(terms, ("z", "yhi"), 0, 0, tiled=True)
    return place(received)


def solution(mesh):
    fine = Mesh(mesh.devices.reshape(SIZES), NAMES)
    corpus = ("z", "yhi", "x")
    query = ("ylo", "core")
    return jax.shard_map(
        per_device,
        mesh=fine,
        in_specs=(P(corpus, query, None), P(query + corpus, None, None), P(query + corpus)),
        out_specs=P(corpus, query),
        check_vma=False,
    )
```

```python
import functools

import jax
import jax.numpy as jnp
from jax import lax
from jax.experimental import pallas as pl
from jax.experimental.pallas import tpu as pltpu
from jax.sharding import Mesh
from jax.sharding import PartitionSpec as P

NAMES = ("ylo", "core", "z", "yhi", "x")
SIZES = (2, 2, 4, 2, 4)
PLANE = ("ylo", "core", "z", "yhi")
OWN, SLOTS, WIDTH = 8, 128, 128
DEPTH = 16
LOWEST = -3.0e38


def plane_pairs(move):
    def index(ylo, core, z, yhi):
        return ((ylo * 2 + core) * 4 + z) * 2 + yhi

    pairs = []
    for ylo in range(2):
        for core in range(2):
            for z in range(4):
                for yhi in range(2):
                    y2, core2, z2 = move(2 * yhi + ylo, core, z)
                    pairs.append((index(ylo, core, z, yhi), index(y2 % 2, core2, z2, y2 // 2)))
    return pairs


def along(first, mask):
    def move(y, core, z):
        if (core == 0) == first:
            return y ^ mask, core, z
        return y, core, z ^ mask

    return plane_pairs(move)


def to_core(v):
    return lax.ppermute(v, "core", [(0, 1), (1, 0)])


def on_x(v, mask, other_mask):
    pairs = [
        (core * 4 + i, core * 4 + (i ^ (mask if core == 0 else other_mask)))
        for core in range(2)
        for i in range(4)
    ]
    return lax.ppermute(v, ("core", "x"), pairs)


def with_lengths(passages, lengths):
    tail = jnp.pad(lengths.astype(passages.dtype), (0, WIDTH - OWN))
    return jnp.concatenate(
        [passages.reshape(OWN * SLOTS, WIDTH), jnp.broadcast_to(tail, (16, WIDTH))], axis=0
    )


def best_dots(rows, places, p_ref, m_ref, s_ref, unit_ref, turns, *acc):
    acc = (acc[:DEPTH], acc[DEPTH:])
    nothing = jnp.zeros((16, 128), jnp.bfloat16)

    def push(g):
        for u in range(2):
            held = jnp.concatenate([ref[j] for ref, j in rows[g][2 * u : 2 * u + 2]], axis=1)
            pltpu.matmul_push_rhs(held, 0, u, transpose=True)

    def issue(unit, j, fresh=False):
        slots = p_ref[pl.ds(pl.multiple_of(unit, 16), 16), :]
        lhs = jnp.concatenate(
            [
                jnp.concatenate([slots, nothing], axis=1),
                jnp.concatenate([nothing, slots], axis=1),
            ],
            axis=0,
        )
        for u in range(2):
            pltpu.matmul_acc_lhs(acc[u][j], lhs, load_staged_rhs=0 if fresh else None)

    def take(unit, j):
        at = lax.shift_right_logical(unit, 7)
        begin = jnp.where(lax.bitwise_and(unit, 127) == 0, 32, at)
        tops = []
        held = [m_ref[b, begin] for b in range(8)]
        for u in range(2):
            d = pltpu.matmul_pop(acc[u][j])
            for half in range(2):
                top = jnp.maximum(d[16 * half : 16 * half + 8], d[16 * half + 8 : 16 * half + 16])
                tops += [top[:, 0:128], top[:, 128:256]]
        for b in range(8):
            m_ref[b, at] = jnp.maximum(held[b], tops[b])

    def turn(t, c):
        for j in range(DEPTH):
            take(unit_ref[t * DEPTH + j], j)
            issue(unit_ref[t * DEPTH + DEPTH + j], j)
        return c

    m_ref[:, 32] = jnp.full((8, 8, 128), LOWEST, jnp.float32)
    rows_ref = m_ref.reshape(8, 264, 128)
    push(0)
    for j in range(DEPTH):
        issue(unit_ref[j], j, fresh=j == 0)
    for g in range(len(rows)):
        lax.fori_loop(0, turns - 1, turn, 0)
        more = g + 1 < len(rows)
        if more:
            push(g + 1)
        last = (turns - 1) * DEPTH
        for j in range(DEPTH):
            take(unit_ref[last + j], j)
            if more:
                issue(unit_ref[j], j, fresh=j == 0)
        for o in range(4):
            for b in range(8):
                top = rows_ref[b, pl.ds(64 * o, 8, stride=8), :]
                for i in range(1, 8):
                    top = jnp.maximum(top, rows_ref[b, pl.ds(64 * o + i, 8, stride=8), :])
                lanes = slice(128 * (b % 2), 128 * (b % 2) + 128)
                s_ref[places[g][b // 2], 8 * o : 8 * o + 8, lanes] += top


def score_kernel(info_ref, *refs):
    rows, pieces, out_ref = refs[:8], refs[8:12], refs[12]
    p_ref, m_ref, s_ref, unit_ref = refs[13:]
    z, yhi, core, x = (info_ref[i] for i in range(4))

    groups, places = [], []
    for k in range(4):
        for j in (0, 2):
            groups.append([(rows[c + k], e) for c in (0, 4) for e in (j, j + 1)])
            by_chain = [[k * 2 + e // 2, e * 2 + k // 2] for e in (j, j + 1)]
            places.append(
                [jnp.where(chain == 0, p, q) for chain in (core, 1 - core) for p, q in by_chain]
            )

    count = jnp.int32(0)
    for m in range(4):
        from_x = lax.bitwise_xor(x, jnp.where(core == 0, (0, 1, 3, 2)[m], (0, 3, 1, 2)[m]))
        p_ref[pl.ds(pl.multiple_of(from_x * 1024, 1024), 1024), :] = pieces[m][0:1024, :]
        lengths = pieces[m][1024:1040, :].astype(jnp.float32)[0:8].astype(jnp.int32)
        units = lax.shift_right_logical(lengths + 15, 4)
        for i in range(OWN):
            for n in range(8):
                unit_ref[count + n] = from_x * 1024 + i * SLOTS + n * 16
            count = count + units[0, i]
            used = units[0, i]
            last = pl.multiple_of(from_x * 1024 + i * SLOTS + (used - 1) * 16, 16)
            both = p_ref[pl.ds(last, 16), :].astype(jnp.float32)
            second = jnp.where(lengths[0, i] == used * 16, both[8:16], both[0:8])
            p_ref[pl.ds(last, 16), :] = jnp.concatenate([both[0:8], second], axis=0).astype(p_ref.dtype)
    for i in range(DEPTH):
        unit_ref[count + i] = unit_ref[count - 1]
    turns = lax.div(count + DEPTH - 1, DEPTH)

    s_ref[...] = jnp.zeros_like(s_ref)
    pl.run_scoped(
        functools.partial(best_dots, groups, places, p_ref, m_ref, s_ref, unit_ref, turns),
        *[pltpu.ACC(u)((32, 256), jnp.float32) for u in range(2) for _ in range(DEPTH)],
    )

    lane = lax.broadcasted_iota(jnp.int32, (32, 256), 1)
    row = lax.broadcasted_iota(jnp.int32, (32, 256), 0)
    pick = jnp.where(lane // 8 == row, 1.0 / 32, 0.0).astype(jnp.bfloat16)
    rest = s_ref[...].reshape(256, 256)
    parts = []
    for _ in range(3):
        parts.append(rest.astype(jnp.bfloat16))
        rest = rest - parts[-1].astype(jnp.float32)

    def add_up(acc):
        for part in parts:
            pltpu.matmul_push_rhs(part, 0, 0, transpose=True)
            pltpu.matmul_acc_lhs(acc, pick, load_staged_rhs=0)
        return pltpu.matmul_pop(acc)

    r = pl.run_scoped(add_up, pltpu.ACC(0)((32, 256), jnp.float32))
    for g in range(8):
        c = r[:, 32 * g : 32 * g + 32]
        place = lax.bitwise_xor(z * 2 + yhi, g)
        out_ref[place] = jnp.concatenate([c[0:8], c[8:16], c[16:24], c[24:32]], axis=1)


def score(info, rows, pieces):
    return pl.pallas_call(
        score_kernel,
        out_shape=jax.ShapeDtypeStruct((8, 8, 128), jnp.float32),
        in_specs=[pl.BlockSpec(memory_space=pltpu.SMEM)]
        + [pl.BlockSpec(memory_space=pltpu.VMEM)] * 12,
        out_specs=pl.BlockSpec(memory_space=pltpu.VMEM),
        scratch_shapes=[
            pltpu.VMEM((4096, 128), jnp.bfloat16),
            pltpu.VMEM((8, 33, 8, 128), jnp.float32),
            pltpu.VMEM((8, 32, 256), jnp.float32),
            pltpu.SMEM((256 + DEPTH,), jnp.int32),
        ],
        compiler_params=pltpu.CompilerParams(vmem_limit_bytes=32 << 20),
    )(info, *rows, *pieces)


def place_kernel(r_ref, o_ref):
    for g in range(4):
        o_ref[8 * g : 8 * g + 8, :] = jnp.concatenate(
            [r_ref[s][:, 32 * g : 32 * g + 32] for s in range(8)], axis=1
        )


def place(received):
    return pl.pallas_call(
        place_kernel,
        out_shape=jax.ShapeDtypeStruct((32, 256), jnp.float32),
        in_specs=[pl.BlockSpec(memory_space=pltpu.VMEM)],
        out_specs=pl.BlockSpec(memory_space=pltpu.VMEM),
    )(received)


def per_device(queries, passages, lengths):
    own = queries.reshape(256, 128)
    info = jnp.stack([lax.axis_index(name) for name in ("z", "yhi", "core", "x")]).astype(jnp.int32)

    near = [own] + [lax.ppermute(own, PLANE, along(True, k)) for k in range(1, 4)]
    filled = with_lengths(passages, lengths)
    once = on_x(filled, 1, 3)
    moved = [filled, once, on_x(filled, 3, 1), on_x(once, 3, 1)]
    block = jnp.stack(near)
    mine = [block] + [lax.ppermute(block, PLANE, along(False, k)) for k in range(1, 4)]
    other = [to_core(v) for v in mine]
    terms = score(info, mine + other, moved)
    received = lax.all_to_all(terms, ("z", "yhi"), 0, 0, tiled=True)
    return place(received)


def solution(mesh):
    fine = Mesh(mesh.devices.reshape(SIZES), NAMES)
    corpus = ("z", "yhi", "x")
    query = ("ylo", "core")
    return jax.shard_map(
        per_device,
        mesh=fine,
        in_specs=(P(corpus, query, None), P(query + corpus, None, None), P(query + corpus)),
        out_specs=P(corpus, query),
        check_vma=False,
    )
```

```python
import functools

import jax
import jax.numpy as jnp
from jax import lax
from jax.experimental import pallas as pl
from jax.experimental.pallas import tpu as pltpu
from jax.sharding import Mesh
from jax.sharding import PartitionSpec as P

NAMES = ("ylo", "core", "z", "yhi", "x")
SIZES = (2, 2, 4, 2, 4)
PLANE = ("ylo", "core", "z", "yhi")
OWN, SLOTS, WIDTH = 8, 128, 128
DEPTH = 16
LOWEST = -3.0e38


def plane_pairs(move):
    def index(ylo, core, z, yhi):
        return ((ylo * 2 + core) * 4 + z) * 2 + yhi

    pairs = []
    for ylo in range(2):
        for core in range(2):
            for z in range(4):
                for yhi in range(2):
                    y2, core2, z2 = move(2 * yhi + ylo, core, z)
                    pairs.append((index(ylo, core, z, yhi), index(y2 % 2, core2, z2, y2 // 2)))
    return pairs


def along(first, mask):
    def move(y, core, z):
        if (core == 0) == first:
            return y ^ mask, core, z
        return y, core, z ^ mask

    return plane_pairs(move)


def to_core(v):
    return lax.ppermute(v, "core", [(0, 1), (1, 0)])


def on_x(v, mask, other_mask):
    pairs = [
        (core * 4 + i, core * 4 + (i ^ (mask if core == 0 else other_mask)))
        for core in range(2)
        for i in range(4)
    ]
    return lax.ppermute(v, ("core", "x"), pairs)


def with_lengths(passages, lengths):
    tail = jnp.pad(lengths.astype(passages.dtype), (0, WIDTH - OWN))
    return jnp.concatenate(
        [passages.reshape(OWN * SLOTS, WIDTH), jnp.broadcast_to(tail, (16, WIDTH))], axis=0
    )


def best_dots(rows, p_ref, m_ref, s_ref, unit_ref, turns, *acc):
    acc = (acc[:DEPTH], acc[DEPTH:])
    nothing = jnp.zeros((16, 128), jnp.bfloat16)

    def push(g):
        for u in range(2):
            held = jnp.concatenate([ref[j] for ref, j in rows[g][2 * u : 2 * u + 2]], axis=1)
            pltpu.matmul_push_rhs(held, 0, u, transpose=True)

    def issue(unit, j, fresh=False):
        slots = p_ref[pl.ds(pl.multiple_of(unit, 16), 16), :]
        lhs = jnp.concatenate(
            [
                jnp.concatenate([slots, nothing], axis=1),
                jnp.concatenate([nothing, slots], axis=1),
            ],
            axis=0,
        )
        for u in range(2):
            pltpu.matmul_acc_lhs(acc[u][j], lhs, load_staged_rhs=0 if fresh else None)

    def take(unit, j):
        at = lax.shift_right_logical(unit, 7)
        begin = jnp.where(lax.bitwise_and(unit, 127) == 0, 32, at)
        tops = []
        held = [m_ref[b, begin] for b in range(8)]
        for u in range(2):
            d = pltpu.matmul_pop(acc[u][j])
            for half in range(2):
                top = jnp.maximum(d[16 * half : 16 * half + 8], d[16 * half + 8 : 16 * half + 16])
                tops += [top[:, 0:128], top[:, 128:256]]
        for b in range(8):
            m_ref[b, at] = jnp.maximum(held[b], tops[b])

    def turn(t, c):
        for j in range(DEPTH):
            take(unit_ref[t * DEPTH + j], j)
            issue(unit_ref[t * DEPTH + DEPTH + j], j)
        return c

    m_ref[:, 32] = jnp.full((8, 8, 128), LOWEST, jnp.float32)
    rows_ref = m_ref.reshape(8, 264, 128)
    push(0)
    for j in range(DEPTH):
        issue(unit_ref[j], j, fresh=j == 0)
    for g in range(len(rows)):
        lax.fori_loop(0, turns - 1, turn, 0)
        more = g + 1 < len(rows)
        if more:
            push(g + 1)
        last = (turns - 1) * DEPTH
        for j in range(DEPTH):
            take(unit_ref[last + j], j)
            if more:
                issue(unit_ref[j], j, fresh=j == 0)
        for o in range(4):
            for b in range(8):
                top = rows_ref[b, pl.ds(64 * o, 8, stride=8), :]
                for i in range(1, 8):
                    top = jnp.maximum(top, rows_ref[b, pl.ds(64 * o + i, 8, stride=8), :])
                lanes = slice(128 * (b % 2), 128 * (b % 2) + 128)
                s_ref[4 * g + b // 2, 8 * o : 8 * o + 8, lanes] = top


def score_kernel(info_ref, *refs):
    rows, pieces, out_ref = refs[:8], refs[8:12], refs[12]
    p_ref, m_ref, s_ref, unit_ref = refs[13:]
    z, yhi, core, x = (info_ref[i] for i in range(4))

    groups = [
        [(rows[c + k], e) for c in (0, 4) for e in (j, j + 1)] for k in range(4) for j in (0, 2)
    ]

    count = jnp.int32(0)
    for m in range(4):
        from_x = lax.bitwise_xor(x, jnp.where(core == 0, (0, 1, 3, 2)[m], (0, 3, 1, 2)[m]))
        p_ref[pl.ds(pl.multiple_of(from_x * 1024, 1024), 1024), :] = pieces[m][0:1024, :]
        lengths = pieces[m][1024:1040, :].astype(jnp.float32)[0:8].astype(jnp.int32)
        units = lax.shift_right_logical(lengths + 15, 4)
        for i in range(OWN):
            for n in range(8):
                unit_ref[count + n] = from_x * 1024 + i * SLOTS + n * 16
            count = count + units[0, i]
            used = units[0, i]
            last = pl.multiple_of(from_x * 1024 + i * SLOTS + (used - 1) * 16, 16)
            both = p_ref[pl.ds(last, 16), :].astype(jnp.float32)
            second = jnp.where(lengths[0, i] == used * 16, both[8:16], both[0:8])
            p_ref[pl.ds(last, 16), :] = jnp.concatenate([both[0:8], second], axis=0).astype(p_ref.dtype)
    for i in range(DEPTH):
        unit_ref[count + i] = unit_ref[count - 1]
    turns = lax.div(count + DEPTH - 1, DEPTH)

    pl.run_scoped(
        functools.partial(best_dots, groups, p_ref, m_ref, s_ref, unit_ref, turns),
        *[pltpu.ACC(u)((32, 256), jnp.float32) for u in range(2) for _ in range(DEPTH)],
    )

    lane = lax.broadcasted_iota(jnp.int32, (32, 256), 1)
    row = lax.broadcasted_iota(jnp.int32, (32, 256), 0)
    pick = jnp.where(lane // 8 == row, 1.0 / 32, 0.0).astype(jnp.bfloat16)
    totals = []
    for dz in range(4):
        for h in range(2):
            places = [(dz * 2 + h) * 4 + core * 2 + e for e in range(2)]
            places += [(k * 2 + dz // 2) * 4 + (1 - core) * 2 + dz % 2 for k in (2 * h, 2 * h + 1)]
            a, b, c, d = (s_ref[i] for i in places)
            totals.append((a + b) + (c + d))
    rest = jnp.concatenate(totals, axis=0)
    parts = []
    for _ in range(3):
        parts.append(rest.astype(jnp.bfloat16))
        rest = rest - parts[-1].astype(jnp.float32)

    def add_up(acc):
        for part in parts:
            pltpu.matmul_push_rhs(part, 0, 0, transpose=True)
            pltpu.matmul_acc_lhs(acc, pick, load_staged_rhs=0)
        return pltpu.matmul_pop(acc)

    r = pl.run_scoped(add_up, pltpu.ACC(0)((32, 256), jnp.float32))
    for g in range(8):
        c = r[:, 32 * g : 32 * g + 32]
        place = lax.bitwise_xor(z * 2 + yhi, g)
        out_ref[place] = jnp.concatenate([c[0:8], c[8:16], c[16:24], c[24:32]], axis=1)


def score(info, rows, pieces):
    return pl.pallas_call(
        score_kernel,
        out_shape=jax.ShapeDtypeStruct((8, 8, 128), jnp.float32),
        in_specs=[pl.BlockSpec(memory_space=pltpu.SMEM)]
        + [pl.BlockSpec(memory_space=pltpu.VMEM)] * 12,
        out_specs=pl.BlockSpec(memory_space=pltpu.VMEM),
        scratch_shapes=[
            pltpu.VMEM((4096, 128), jnp.bfloat16),
            pltpu.VMEM((8, 33, 8, 128), jnp.float32),
            pltpu.VMEM((32, 32, 256), jnp.float32),
            pltpu.SMEM((256 + DEPTH,), jnp.int32),
        ],
        compiler_params=pltpu.CompilerParams(vmem_limit_bytes=32 << 20),
    )(info, *rows, *pieces)


def place_kernel(r_ref, o_ref):
    for g in range(4):
        o_ref[8 * g : 8 * g + 8, :] = jnp.concatenate(
            [r_ref[s][:, 32 * g : 32 * g + 32] for s in range(8)], axis=1
        )


def place(received):
    return pl.pallas_call(
        place_kernel,
        out_shape=jax.ShapeDtypeStruct((32, 256), jnp.float32),
        in_specs=[pl.BlockSpec(memory_space=pltpu.VMEM)],
        out_specs=pl.BlockSpec(memory_space=pltpu.VMEM),
    )(received)


def per_device(queries, passages, lengths):
    own = queries.reshape(256, 128)
    info = jnp.stack([lax.axis_index(name) for name in ("z", "yhi", "core", "x")]).astype(jnp.int32)

    near = [own] + [lax.ppermute(own, PLANE, along(True, k)) for k in range(1, 4)]
    filled = with_lengths(passages, lengths)
    once = on_x(filled, 1, 3)
    moved = [filled, once, on_x(filled, 3, 1), on_x(once, 3, 1)]
    block = jnp.stack(near)
    mine = [block] + [lax.ppermute(block, PLANE, along(False, k)) for k in range(1, 4)]
    other = [to_core(v) for v in mine]
    terms = score(info, mine + other, moved)
    received = lax.all_to_all(terms, ("z", "yhi"), 0, 0, tiled=True)
    return place(received)


def solution(mesh):
    fine = Mesh(mesh.devices.reshape(SIZES), NAMES)
    corpus = ("z", "yhi", "x")
    query = ("ylo", "core")
    return jax.shard_map(
        per_device,
        mesh=fine,
        in_specs=(P(corpus, query, None), P(query + corpus, None, None), P(query + corpus)),
        out_specs=P(corpus, query),
        check_vma=False,
    )
```

```python
import functools

import jax
import jax.numpy as jnp
from jax import lax
from jax.experimental import pallas as pl
from jax.experimental.pallas import tpu as pltpu
from jax.sharding import Mesh
from jax.sharding import PartitionSpec as P

NAMES = ("ylo", "core", "z", "yhi", "x")
SIZES = (2, 2, 4, 2, 4)
PLANE = ("ylo", "core", "z", "yhi")
OWN, SLOTS, WIDTH = 8, 128, 128
DEPTH = 16
LOWEST = -3.0e38


def plane_pairs(move):
    def index(ylo, core, z, yhi):
        return ((ylo * 2 + core) * 4 + z) * 2 + yhi

    pairs = []
    for ylo in range(2):
        for core in range(2):
            for z in range(4):
                for yhi in range(2):
                    y2, core2, z2 = move(2 * yhi + ylo, core, z)
                    pairs.append((index(ylo, core, z, yhi), index(y2 % 2, core2, z2, y2 // 2)))
    return pairs


def along(first, mask):
    def move(y, core, z):
        if (core == 0) == first:
            return y ^ mask, core, z
        return y, core, z ^ mask

    return plane_pairs(move)


def to_core(v):
    return lax.ppermute(v, "core", [(0, 1), (1, 0)])


def on_x(v, mask, other_mask):
    pairs = [
        (core * 4 + i, core * 4 + (i ^ (mask if core == 0 else other_mask)))
        for core in range(2)
        for i in range(4)
    ]
    return lax.ppermute(v, ("core", "x"), pairs)


def with_lengths(passages, lengths):
    tail = jnp.pad(lengths.astype(passages.dtype), (0, WIDTH - OWN))
    return jnp.concatenate(
        [passages.reshape(OWN * SLOTS, WIDTH), jnp.broadcast_to(tail, (16, WIDTH))], axis=0
    )


def best_dots(rows, p_ref, m_ref, s_ref, unit_ref, turns, *acc):
    acc = (acc[:DEPTH], acc[DEPTH:])
    nothing = jnp.zeros((16, 128), jnp.bfloat16)

    def push(g):
        for u in range(2):
            held = jnp.concatenate([ref[j] for ref, j in rows[g][2 * u : 2 * u + 2]], axis=1)
            pltpu.matmul_push_rhs(held, 0, u, transpose=True)

    def issue(unit, j, fresh=False):
        slots = p_ref[pl.ds(pl.multiple_of(unit, 16), 16), :]
        lhs = jnp.concatenate(
            [
                jnp.concatenate([slots, nothing], axis=1),
                jnp.concatenate([nothing, slots], axis=1),
            ],
            axis=0,
        )
        for u in range(2):
            pltpu.matmul_acc_lhs(acc[u][j], lhs, load_staged_rhs=0 if fresh else None)

    def take(unit, j):
        at = lax.shift_right_logical(unit, 7)
        begin = jnp.where(lax.bitwise_and(unit, 127) == 0, 32, at)
        tops = []
        held = [m_ref[b, begin] for b in range(8)]
        for u in range(2):
            d = pltpu.matmul_pop(acc[u][j])
            for half in range(2):
                top = jnp.maximum(d[16 * half : 16 * half + 8], d[16 * half + 8 : 16 * half + 16])
                tops += [top[:, 0:128], top[:, 128:256]]
        for b in range(8):
            m_ref[b, at] = jnp.maximum(held[b], tops[b])

    def turn(t, c):
        for j in range(DEPTH):
            take(unit_ref[t * DEPTH + j], j)
            issue(unit_ref[t * DEPTH + DEPTH + j], j)
        return c

    m_ref[:, 32] = jnp.full((8, 8, 128), LOWEST, jnp.float32)
    rows_ref = m_ref.reshape(8, 264, 128)
    push(0)
    for j in range(DEPTH):
        issue(unit_ref[j], j, fresh=j == 0)
    for g in range(len(rows)):
        lax.fori_loop(0, turns - 1, turn, 0)
        more = g + 1 < len(rows)
        if more:
            push(g + 1)
        last = (turns - 1) * DEPTH
        for j in range(DEPTH):
            take(unit_ref[last + j], j)
            if more:
                issue(unit_ref[j], j, fresh=j == 0)
        for o in range(4):
            for b in range(8):
                top = rows_ref[b, pl.ds(64 * o, 8, stride=8), :]
                for i in range(1, 8):
                    top = jnp.maximum(top, rows_ref[b, pl.ds(64 * o + i, 8, stride=8), :])
                lanes = slice(128 * (b % 2), 128 * (b % 2) + 128)
                s_ref[4 * g + b // 2, 8 * o : 8 * o + 8, lanes] = top


def score_kernel(info_ref, *refs):
    rows, pieces, out_ref = refs[:8], refs[8:12], refs[12]
    p_ref, m_ref, s_ref, unit_ref = refs[13:]
    z, yhi, core, x = (info_ref[i] for i in range(4))

    groups = [
        [(rows[c + k], e) for c in (0, 4) for e in (j, j + 1)] for k in range(4) for j in (0, 2)
    ]

    count = jnp.int32(0)
    for m in range(4):
        from_x = lax.bitwise_xor(x, jnp.where(core == 0, (0, 1, 3, 2)[m], (0, 3, 1, 2)[m]))
        p_ref[pl.ds(pl.multiple_of(from_x * 1024, 1024), 1024), :] = pieces[m][0:1024, :]
        lengths = pieces[m][1024:1040, :].astype(jnp.float32)[0:8].astype(jnp.int32)
        units = lax.shift_right_logical(lengths + 15, 4)
        for i in range(OWN):
            for n in range(8):
                unit_ref[count + n] = from_x * 1024 + i * SLOTS + n * 16
            count = count + units[0, i]
            used = units[0, i]
            last = pl.multiple_of(from_x * 1024 + i * SLOTS + (used - 1) * 16, 16)
            both = p_ref[pl.ds(last, 16), :].astype(jnp.float32)
            second = jnp.where(lengths[0, i] == used * 16, both[8:16], both[0:8])
            p_ref[pl.ds(last, 16), :] = jnp.concatenate([both[0:8], second], axis=0).astype(p_ref.dtype)
    for i in range(DEPTH):
        unit_ref[count + i] = unit_ref[count - 1]
    turns = lax.div(count + DEPTH - 1, DEPTH)

    pl.run_scoped(
        functools.partial(best_dots, groups, p_ref, m_ref, s_ref, unit_ref, turns),
        *[pltpu.ACC(u)((32, 256), jnp.float32) for u in range(2) for _ in range(DEPTH)],
    )

    lane = lax.broadcasted_iota(jnp.int32, (32, 256), 1)
    row = lax.broadcasted_iota(jnp.int32, (32, 256), 0)
    pick = jnp.where(lane // 8 == row, 1.0 / 32, 0.0).astype(jnp.bfloat16)
    totals = []
    for dz in range(4):
        for h in range(2):
            places = [(dz * 2 + h) * 4 + core * 2 + e for e in range(2)]
            places += [(k * 2 + dz // 2) * 4 + (1 - core) * 2 + dz % 2 for k in (2 * h, 2 * h + 1)]
            a, b, c, d = (s_ref[i] for i in places)
            totals.append((a + b) + (c + d))
    rest = jnp.concatenate(totals, axis=0)
    parts = []
    for _ in range(3):
        parts.append(rest.astype(jnp.bfloat16))
        rest = rest - parts[-1].astype(jnp.float32)

    def add_up(acc):
        for part in parts:
            pltpu.matmul_push_rhs(part, 0, 0, transpose=True)
            pltpu.matmul_acc_lhs(acc, pick, load_staged_rhs=0)
        return pltpu.matmul_pop(acc)

    r = pl.run_scoped(add_up, pltpu.ACC(0)((32, 256), jnp.float32))
    for g in range(8):
        c = r[:, 32 * g : 32 * g + 32]
        place = lax.bitwise_xor(z * 2 + yhi, g)
        out_ref[place] = jnp.concatenate([c[0:8], c[8:16], c[16:24], c[24:32]], axis=1)


def score(info, rows, pieces):
    return pl.pallas_call(
        score_kernel,
        out_shape=jax.ShapeDtypeStruct((8, 8, 128), jnp.float32),
        in_specs=[pl.BlockSpec(memory_space=pltpu.SMEM)]
        + [pl.BlockSpec(memory_space=pltpu.VMEM)] * 12,
        out_specs=pl.BlockSpec(memory_space=pltpu.VMEM),
        scratch_shapes=[
            pltpu.VMEM((4096, 128), jnp.bfloat16),
            pltpu.VMEM((8, 33, 8, 128), jnp.float32),
            pltpu.VMEM((32, 32, 256), jnp.float32),
            pltpu.SMEM((256 + DEPTH,), jnp.int32),
        ],
        compiler_params=pltpu.CompilerParams(vmem_limit_bytes=32 << 20),
    )(info, *rows, *pieces)


def place_kernel(r_ref, o_ref):
    for g in range(4):
        o_ref[8 * g : 8 * g + 8, :] = jnp.concatenate(
            [r_ref[s][:, 32 * g : 32 * g + 32] for s in range(8)], axis=1
        )


def place(received):
    return pl.pallas_call(
        place_kernel,
        out_shape=jax.ShapeDtypeStruct((32, 256), jnp.float32),
        in_specs=[pl.BlockSpec(memory_space=pltpu.VMEM)],
        out_specs=pl.BlockSpec(memory_space=pltpu.VMEM),
    )(received)


def in_order(send):
    sent = {k: send(k) for k in (1, 3, 2)}
    return [sent[k] for k in (1, 2, 3)]


def per_device(queries, passages, lengths):
    own = queries.reshape(256, 128)
    info = jnp.stack([lax.axis_index(name) for name in ("z", "yhi", "core", "x")]).astype(jnp.int32)

    near = [own] + in_order(lambda k: lax.ppermute(own, PLANE, along(True, k)))
    filled = with_lengths(passages, lengths)
    once = on_x(filled, 1, 3)
    moved = [filled, once, on_x(filled, 3, 1), on_x(once, 3, 1)]
    block = jnp.stack(near)
    mine = [block] + in_order(lambda k: lax.ppermute(block, PLANE, along(False, k)))
    other = [to_core(v) for v in mine]
    terms = score(info, mine + other, moved)
    received = lax.all_to_all(terms, ("z", "yhi"), 0, 0, tiled=True)
    return place(received)


def solution(mesh):
    fine = Mesh(mesh.devices.reshape(SIZES), NAMES)
    corpus = ("z", "yhi", "x")
    query = ("ylo", "core")
    return jax.shard_map(
        per_device,
        mesh=fine,
        in_specs=(P(corpus, query, None), P(query + corpus, None, None), P(query + corpus)),
        out_specs=P(corpus, query),
        check_vma=False,
    )
```
